32 devices in a mesh: row: 2 (over core), col: 16 (over z, y, x).
Axes of the slice: x: 2, y: 2, z: 4, core: 2. Of those that a mesh axis runs over, the one named last changes fastest.
Arguments:
- pair: bfloat16 [192, 192, 128], P('row', 'col'), may hold values from -6 to 6
- seq: bfloat16 [192, 1024], P(None, 'col'), may hold values from -6 to 6
- w_hidden: bfloat16 [128, 512], replicated, may hold values from -0.5 to 0.5
- w_back: bfloat16 [512, 128], replicated, may hold values from -0.25 to 0.25
- w_bias: bfloat16 [128, 32], replicated, may hold values from -0.5 to 0.5
- w_query: bfloat16 [1024, 1024], replicated, may hold values from -10 to 10
- w_key: bfloat16 [1024, 1024], replicated, may hold values from -0.1875 to 0.1875
- w_value: bfloat16 [1024, 1024], replicated, may hold values from -0.1875 to 0.1875
- w_out: bfloat16 [1024, 1024], replicated, may hold values from -0.1875 to 0.1875
- w_project: bfloat16 [1024, 128], replicated, may hold values from -0.1875 to 0.1875
- w_pair: bfloat16 [128, 128], replicated, may hold values from -0.5 to 0.5
Outputs:
- pair_out: bfloat16 [192, 192, 128], P('row', 'col')
- seq_new: bfloat16 [192, 1024], P('row', 'col')
The draws below stay inside these ranges and needn't reach their ends.
All inputs are finite; a program needn't handle non-finite values.
Results may differ from the reference program's by a relative error of at most 0.013.
The reference program's roundings to bfloat16 on the way count: a program that leaves them out, or rounds other values in their place, can miss the bound.
Values may be sent and summed in bfloat16 or wider, within the bound.
No kernel may reach another device: no remote copies, remote signals or barrier semaphores. Data moves between devices by JAX's collectives and lax.ppermute only.
A program may use at most 128 MiB of HBM per device.

```python
import jax
import jax.numpy as jnp
from jax import lax

D = 1024
HEADS = 32
C = 128
PH = 512
L = 192
N_ROW = 2


def draw_w_query(key, part):
    base = jax.random.truncated_normal(key, -4.0, 4.0, (D, D), jnp.float32) * D ** (-0.5)
    return base.astype(jnp.bfloat16)


def block_scale(stream_key, shape, shards, smallest, top_value):
    def one(dim, shards_of):
        heights = jax.random.uniform(jax.random.fold_in(jax.random.fold_in(stream_key, 6), dim), (shards_of,), jnp.float32, smallest / len(shards), top_value / len(shards))
        return jnp.repeat(jnp.exp(heights), shape[dim] // shards_of).reshape((-1,) + (1,) * (len(shape) - dim - 1))

    level = one(*shards[0])
    for cut in shards[1:]:
        level = level * one(*cut)
    return level


def scatter_about(stream_key, extent, width, reach, cuts=(), held_as=jnp.bfloat16):
    array = jax.random.normal(stream_key, extent, jnp.float32) * width
    if len(cuts) > 0:
        array = block_scale(stream_key, extent, cuts, -0.22, 0.18) * array
    return jnp.clip(array, min=-reach, max=reach).astype(held_as)


def setup_inputs(seed: int = 0) -> dict:
    seeds = jax.random.split(jax.random.key(seed), 12)
    pair = scatter_about(seeds[0], (L, L, C), 1.0, 6.0, ((0, 2), (1, 16)))
    seq = scatter_about(seeds[1], (L, D), 1.0, 6.0, ((1, 16),))
    w_hidden = scatter_about(seeds[2], (C, PH), C ** -0.5, 0.5)
    w_back = scatter_about(seeds[3], (PH, C), PH ** -0.5, 0.25)
    w_bias = scatter_about(seeds[4], (C, HEADS), C ** -0.5, 0.5)
    w_query = draw_w_query(jax.random.fold_in(seeds[11], 71), 0)
    w_key = scatter_about(seeds[6], (D, D), D ** -0.5, 0.1875)
    w_value = scatter_about(seeds[7], (D, D), D ** -0.5, 0.1875)
    w_out = scatter_about(seeds[8], (D, D), D ** -0.5, 0.1875)
    w_project = scatter_about(seeds[9], (D, C), D ** -0.5, 0.1875)
    w_pair = scatter_about(seeds[10], (C, C), C ** -0.5, 0.5)
    return dict(pair=pair, seq=seq, w_hidden=w_hidden, w_back=w_back, w_bias=w_bias, w_query=w_query, w_key=w_key, w_value=w_value, w_out=w_out, w_project=w_project, w_pair=w_pair)


eps_norm = 1e-05

def layer_norm(values_in):
    row_mean = lax.optimization_barrier(jnp.mean(values_in, axis=-1, keepdims=True))
    centred = values_in - row_mean
    row_var = lax.optimization_barrier(jnp.mean(centred * centred, axis=-1, keepdims=True))
    return centred * lax.rsqrt(row_var + eps_norm)

def reference(pair, seq, w_hidden, w_back, w_bias, w_query, w_key, w_value, w_out, w_project, w_pair):
    f32 = jnp.float32
    bf16 = jnp.bfloat16
    highest = lax.Precision.HIGHEST
    row_span = L // N_ROW
    head_dim = D // HEADS
    half = C // 2
    seq_norm = layer_norm(seq.astype(f32)).astype(bf16)
    queries = jnp.dot(seq_norm, w_query, preferred_element_type=f32).astype(bf16)
    keys_proj = jnp.dot(seq_norm, w_key, preferred_element_type=f32).astype(bf16)
    values_proj = jnp.dot(seq_norm, w_value, preferred_element_type=f32).astype(bf16)
    keys_f = keys_proj.astype(f32).reshape(L, HEADS, head_dim)
    values_f = values_proj.astype(f32).reshape(L, HEADS, head_dim)

    def first_pass(inputs):
        pair_rows, query_rows, seq_rows = inputs
        normed = layer_norm(pair_rows.astype(f32)).astype(bf16).reshape(-1, C)
        hidden = jax.nn.relu(jnp.dot(normed, w_hidden, preferred_element_type=f32)).astype(bf16)
        pair_mid = (pair_rows.astype(f32) + jnp.dot(hidden, w_back, preferred_element_type=f32).reshape(row_span, L, C)).astype(bf16)
        mid_norm = layer_norm(pair_mid.astype(f32)).astype(bf16).reshape(-1, C)
        pair_bias = jnp.dot(mid_norm, w_bias, preferred_element_type=f32).reshape(row_span, L, HEADS).transpose(2, 0, 1)
        query_f = query_rows.astype(f32).reshape(row_span, HEADS, head_dim)
        scores = jnp.einsum('ihd,jhd->hij', query_f, keys_f, precision=highest) * head_dim ** (-0.5) + pair_bias
        row_top = lax.optimization_barrier(jnp.max(scores, axis=2, keepdims=True))
        weights = jnp.exp(scores - row_top)
        denom_sum = lax.optimization_barrier(jnp.sum(weights, axis=2))
        weighted = jnp.einsum('hij,jhd->ihd', weights, values_f, precision=highest)
        attended = (weighted / denom_sum.T[:, :, None]).reshape(row_span, D).astype(bf16)
        seq_next = (seq_rows.astype(f32) + jnp.dot(attended, w_out, preferred_element_type=f32)).astype(bf16)
        projected = jnp.dot(layer_norm(seq_next.astype(f32)).astype(bf16), w_project, preferred_element_type=f32).astype(bf16)
        return (pair_mid, seq_next, projected)
    pair_mid, seq_next, projected = lax.map(first_pass, (pair.reshape(N_ROW, row_span, L, C), queries.reshape(N_ROW, row_span, D), seq.reshape(N_ROW, row_span, D)))
    right_proj = projected.reshape(L, C)[:, half:].astype(f32)

    def second_pass(inputs):
        mid_rows, proj_rows = inputs
        left_proj = proj_rows[:, :half].astype(f32)
        product = left_proj[:, None, :] * right_proj[None, :, :]
        difference = left_proj[:, None, :] - right_proj[None, :, :]
        feature = jnp.concatenate([product, difference], axis=-1).astype(bf16).reshape(-1, C)
        return (mid_rows.astype(f32) + jnp.dot(feature, w_pair, preferred_element_type=f32).reshape(row_span, L, C)).astype(bf16)
    pair_out = lax.map(second_pass, (pair_mid, projected)).reshape(L, L, C)
    return (pair_out, seq_next.reshape(L, D))
```

```python
import functools

import jax
import jax.numpy as jnp
from jax import lax
from jax.experimental import pallas as pl
from jax.experimental.pallas import tpu as pltpu
from jax.sharding import PartitionSpec as P

HEADS = 32
LANES = 128
eps_norm = 1e-05
f32 = jnp.float32
bf16 = jnp.bfloat16


def layer_norm(values_in):
    row_mean = jnp.mean(values_in, axis=-1, keepdims=True)
    centred = values_in - row_mean
    row_var = jnp.mean(centred * centred, axis=-1, keepdims=True)
    return centred * lax.rsqrt(row_var + eps_norm)


def dot(a, b):
    return jnp.dot(a, b, preferred_element_type=f32)


def dot_nt(a, b):
    return lax.dot_general(a, b, (((1,), (1,)), ((), ())), preferred_element_type=f32)


def round_up(n, m):
    return -(-n // m) * m


def one_hot_rows(shape, target):
    rows = lax.broadcasted_iota(jnp.int32, shape, 0)
    cols = lax.broadcasted_iota(jnp.int32, shape, 1)
    return (cols == target(rows)).astype(f32).astype(bf16)


def call(kernel, outs, args, scratch=(), flops=1000):
    vmem = pl.BlockSpec(memory_space=pltpu.VMEM)
    size = sum(round_up(a.size * a.dtype.itemsize, 4096) for a in args)
    size += sum(a.size * a.dtype.itemsize for a in outs)
    return pl.pallas_call(
        kernel,
        out_shape=outs,
        in_specs=[vmem] * len(args),
        out_specs=tuple(vmem for _ in outs),
        scratch_shapes=list(scratch),
        compiler_params=pltpu.CompilerParams(vmem_limit_bytes=56 * 1024 * 1024),
        cost_estimate=pl.CostEstimate(flops=flops, bytes_accessed=size, transcendentals=0),
    )(*args)


def pack_seq(n_row, rows, seq_ref, out_ref):
    feats = seq_ref.shape[0]
    fold = LANES // feats
    short = rows // fold
    row = lax.axis_index("row")
    for v in range(n_row):

        @pl.when(row == v)
        def _():
            parts = [
                seq_ref[:, v * rows + p * short : v * rows + (p + 1) * short].astype(f32)
                for p in range(fold)
            ]
            tile = jnp.concatenate(parts, axis=0).T.astype(bf16)
            out_ref[...] = jnp.broadcast_to(tile[None], out_ref.shape)


def bias_plan(rows, cols, n_col):
    own = rows // n_col
    keys = round_up(cols, 16)
    per_tile = LANES // HEADS
    full, rest = divmod(own, per_tile)
    split = per_tile // rest if rest and per_tile % rest == 0 else 1
    if rest and (keys // split) % 8:
        split = 1
    height = full * keys + (keys // split if rest else 0)
    return own, keys, full, rest, split, height


def transition(n_col, chunk, pair_ref, hidden_ref, back_ref, bias_ref, mid_ref, msg_ref, norm_ref):
    cols, rows, chans = pair_ref.shape
    own, keys, full, rest, split, _ = bias_plan(rows, cols, n_col)
    per_tile = LANES // HEADS
    if keys > cols:
        norm_ref[cols * rows :, :] = jnp.zeros(((keys - cols) * rows, chans), f32)

    def step(t):
        at = t * chunk
        pair = pair_ref[pl.ds(at, chunk)].reshape(chunk * rows, chans).astype(f32)
        normed = layer_norm(pair).astype(bf16)
        hidden = jnp.maximum(dot(normed, hidden_ref[...]), 0.0).astype(bf16)
        mid = (pair + dot(hidden, back_ref[...])).astype(bf16)
        mid_ref[pl.ds(at, chunk)] = mid.reshape(chunk, rows, chans)
        start = at * rows if isinstance(at, int) else pl.multiple_of(at * rows, 8)
        norm_ref[pl.ds(start, chunk * rows), :] = layer_norm(mid.astype(f32))

    if cols // chunk <= 4:
        for t in range(cols // chunk):
            step(t)
    else:
        pl.loop(0, cols // chunk)(step)

    w_t = bias_ref[...]
    zero = jnp.zeros_like(w_t)
    placed = [
        jnp.concatenate([w_t if k == p else zero for k in range(per_tile)], axis=0)
        for p in range(per_tile)
    ]

    def queries(q):
        parts = [norm_ref[pl.ds(c * own + q, keys, stride=rows), :] for c in range(n_col)]
        return jnp.concatenate(parts, axis=0)

    for tile in range(full):
        wide = jnp.concatenate(
            [queries(tile * per_tile + p).astype(bf16) for p in range(per_tile)], axis=1
        )
        acc = dot_nt(wide, jnp.concatenate(placed, axis=1))
        msg_ref[:, tile * keys : (tile + 1) * keys, :] = acc.reshape(n_col, keys, LANES)
    if rest:
        small = keys // split
        lhs, rhs = [], []
        for p in range(rest):
            q_rows = queries(full * per_tile + p).reshape(n_col, split, small, chans)
            for s in range(split):
                lhs.append(q_rows[:, s].reshape(n_col * small, chans).astype(bf16))
                rhs.append(placed[s * rest + p])
        acc = dot_nt(jnp.concatenate(lhs, axis=1), jnp.concatenate(rhs, axis=1))
        msg_ref[:, full * keys :, :] = acc.reshape(n_col, small, LANES)


def project_qkv(n_row, rows, own, *refs):
    n_in = 2 if n_row == 2 else 1
    seq_refs = refs[:n_in]
    wq_ref, wk_ref, wv_ref, k_ref, v_ref, qm_ref, own_ref, x_ref, xn_ref = refs[n_in:]
    n_col, short, _ = seq_refs[0].shape[-3:]
    width = x_ref.shape[1]
    feats = width // n_col
    fold = LANES // feats
    head_dim = width // HEADS
    length = x_ref.shape[0]
    row, col = lax.axis_index("row"), lax.axis_index("col")
    slot = lax.broadcasted_iota(jnp.int32, (short, LANES), 1) // feats

    def place(read, v):
        for g in range(width // LANES):
            got = [read(fold * g + s).astype(f32) for s in range(fold)]
            for p in range(fold):
                piece = got[p]
                for s in range(fold):
                    if s != p:
                        piece = jnp.where(
                            slot == s, pltpu.roll(got[s], (s - p) % fold * feats, 1), piece
                        )
                start = v * rows + p * short
                if not isinstance(start, int):
                    start = pl.multiple_of(start, 16)
                x_ref[pl.ds(start, short), g * LANES : (g + 1) * LANES] = piece

    if n_row == 2:
        place(lambda c: seq_refs[0][c], row)
        place(lambda c: seq_refs[1][c], 1 - row)
    else:
        pl.loop(0, n_row)(lambda v: place(lambda c: seq_refs[0][v, c], v))

    block = rows * (2 if n_row == 2 else 1)

    def step(b):
        start = b * block if isinstance(b, int) else pl.multiple_of(b * block, 16)
        at = pl.ds(start, block)
        normed = layer_norm(x_ref[at, :]).astype(bf16)
        xn_ref[at, :] = normed
        k_ref[at, :] = dot(normed, wk_ref[...]).astype(bf16)
        v_ref[at, :] = dot(normed, wv_ref[...]).astype(bf16)

    if length == block:
        step(0)
    else:
        pl.loop(0, length // block)(step)

    padded = own_ref.shape[0]
    pick = one_hot_rows((padded, length), lambda i: row * rows + col * own + i)
    own_ref[...] = dot(pick, x_ref[...].astype(bf16))
    queries = dot(dot(pick, xn_ref[...]).astype(bf16), wq_ref[...]).astype(bf16)
    spread = one_hot_rows((padded * HEADS, padded), lambda ih: ih // HEADS)
    wide = dot(spread, queries)
    head_of_row = lax.broadcasted_iota(jnp.int32, wide.shape, 0) % HEADS
    head_of_lane = lax.broadcasted_iota(jnp.int32, wide.shape, 1) // head_dim
    qm_ref[...] = jnp.where(head_of_row == head_of_lane, wide, 0.0).astype(bf16)


def attend(plan, cols, fold, msg_ref, k_ref, v_ref, qm_ref, own_ref, wo_ref, wp_ref, out_ref, bias_ref):
    own, keys, full, rest, split, _ = plan
    n_col = msg_ref.shape[0]
    length, width = k_ref.shape
    head_dim = width // HEADS
    padded = own_ref.shape[0]
    small = keys // split
    for c in range(n_col):
        for tile in range(full):
            bias_ref[c * cols : (c + 1) * cols, tile * LANES : (tile + 1) * LANES] = msg_ref[
                c, tile * keys : tile * keys + cols, :
            ]
        if rest:
            last = msg_ref[c, full * keys :, :]
            for s in range(split):
                height = min(small, cols - s * small)
                if height <= 0:
                    continue
                moved = last
                if s:
                    moved = pltpu.roll(last, LANES - s * rest * HEADS, 1)
                bias_ref[c * cols + s * small : c * cols + s * small + height, full * LANES :] = (
                    moved[:height]
                )
    scores = dot_nt(k_ref[...], qm_ref[...]) * head_dim ** (-0.5) + bias_ref[...]
    top = jnp.max(scores, axis=0, keepdims=True)
    weights = jnp.exp(scores - top)
    denom = jnp.sum(weights, axis=0, keepdims=True)
    by_query = (weights / denom).T
    high = by_query.astype(bf16)
    low = (by_query - high.astype(f32)).astype(bf16)
    values = v_ref[...]
    mixed = dot(high, values) + dot(low, values)
    head_of_row = lax.broadcasted_iota(jnp.int32, mixed.shape, 0) % HEADS
    head_of_lane = lax.broadcasted_iota(jnp.int32, mixed.shape, 1) // head_dim
    mixed = jnp.where(head_of_row == head_of_lane, mixed, 0.0)
    attended = jnp.sum(mixed.reshape(padded, HEADS, width), axis=1).astype(bf16)
    seq_next = (own_ref[...] + dot(attended, wo_ref[...])).astype(bf16)
    seq_wide = seq_next.astype(f32)
    projected = dot(layer_norm(seq_wide).astype(bf16), wp_ref[...]).astype(bf16).astype(f32)
    n_row = out_ref.shape[0]
    for g in range(width // LANES):
        tile = jnp.concatenate([projected, seq_wide[:, g * LANES : (g + 1) * LANES]], axis=0)
        out_ref[:, fold * g : fold * (g + 1)] = jnp.broadcast_to(
            tile.astype(bf16)[None, None], (n_row, fold) + tile.shape
        )


def update_pair(own, fold, msg_ref, mid_ref, wpair_ref, pair_ref, seq_ref, left_ref, slab_ref):
    cols, rows, chans = mid_ref.shape
    n_row, n_col, twice, _ = msg_ref.shape
    padded = twice // 2
    half = chans // 2
    row, col = lax.axis_index("row"), lax.axis_index("col")
    for c in range(n_col):
        block = msg_ref[row, c].astype(f32)
        left_ref[c * own : (c + 1) * own, :] = block[:own]
        slab_ref[c * own : (c + 1) * own, :] = block[padded : padded + own]
    feats = LANES // fold
    turned = slab_ref[...].T
    for s in range(fold):

        @pl.when(lax.rem(col, fold) == s)
        def _():
            seq_ref[...] = turned[s * feats : (s + 1) * feats].astype(bf16)

    both = left_ref[...]
    is_first = lax.broadcasted_iota(jnp.int32, (1, chans), 1) < half
    left = jnp.where(is_first, both, pltpu.roll(both, half, 1))
    blocks_each = cols // own
    first = col * blocks_each

    def step(t):
        at = first + t
        theirs = msg_ref[at // n_col, lax.rem(at, n_col)].astype(f32)[:padded]
        right = jnp.where(is_first, pltpu.roll(theirs, half, 1), theirs)
        feature = []
        for i in range(own):
            r = right[i : i + 1]
            feature.append(jnp.where(is_first, left * r, left - r).astype(bf16))
        out = dot(jnp.concatenate(feature, axis=0), wpair_ref[...])
        here = pl.ds(t * own, own)
        mid = mid_ref[here].astype(f32)
        pair_ref[here] = (mid + out.reshape(own, rows, chans)).astype(bf16)

    if blocks_each <= 4:
        for t in range(blocks_each):
            step(t)
    else:
        pl.loop(0, blocks_each)(step)


def local(pair, seq, w_hidden, w_back, w_bias, w_query, w_key, w_value, w_out, w_project, w_pair):
    shape = jax.ShapeDtypeStruct
    rows, cols, chans = pair.shape
    length, feats = seq.shape
    width = w_query.shape[0]
    n_row, n_col = lax.axis_size("row"), lax.axis_size("col")
    fold = LANES // feats
    short = rows // fold
    plan = bias_plan(rows, cols, n_col)
    own, keys, full, rest, _, height = plan
    padded = round_up(own, 8)
    hidden_units = w_hidden.shape[1]

    (seq_msg,) = call(
        functools.partial(pack_seq, n_row, rows), (shape((n_col, short, LANES), bf16),), (seq.T,)
    )
    seq_rows = lax.all_to_all(seq_msg, "col", split_axis=0, concat_axis=0, tiled=True)
    if n_row == 2:
        seq_parts = (seq_rows, lax.ppermute(seq_rows, "row", [(0, 1), (1, 0)]))
    else:
        seq_parts = (lax.all_gather(seq_rows, "row"),)

    chunk = max(k for k in range(1, cols + 1) if cols % k == 0 and k * rows <= 576)
    pair_mid, bias_msg = call(
        functools.partial(transition, n_col, chunk),
        (shape((cols, rows, chans), bf16), shape((n_col, height, LANES), f32)),
        (pair.transpose(1, 0, 2), w_hidden, w_back, w_bias.T),
        [pltpu.VMEM((keys * rows, chans), f32)],
        flops=4 * rows * cols * chans * hidden_units,
    )
    bias_rows = lax.all_to_all(bias_msg, "col", split_axis=0, concat_axis=0, tiled=True)

    keys_proj, values_proj, queries, own_seq = call(
        functools.partial(project_qkv, n_row, rows, own),
        (
            shape((length, width), bf16),
            shape((length, width), bf16),
            shape((padded * HEADS, width), bf16),
            shape((padded, width), f32),
        ),
        seq_parts + (w_query, w_key, w_value),
        [pltpu.VMEM((length, width), f32), pltpu.VMEM((length, width), bf16)],
        flops=4 * length * width * width,
    )
    (out_msg,) = call(
        functools.partial(attend, plan, cols, fold),
        (shape((n_row, n_col, 2 * padded, LANES), bf16),),
        (bias_rows, keys_proj, values_proj, queries, own_seq, w_out, w_project),
        [pltpu.VMEM((length, padded * HEADS), f32)],
        flops=6 * length * padded * HEADS * width,
    )
    flat = out_msg.reshape(n_row * n_col, 2 * padded, LANES)
    got = lax.all_to_all(flat, ("row", "col"), split_axis=0, concat_axis=0, tiled=True)
    pair_out, seq_out = call(
        functools.partial(update_pair, own, fold),
        (shape((cols, rows, chans), bf16), shape((feats, rows), bf16)),
        (got.reshape(out_msg.shape), pair_mid, w_pair),
        [pltpu.VMEM((rows, LANES), f32), pltpu.VMEM((rows, LANES), f32)],
        flops=2 * rows * cols * chans * chans,
    )
    return (pair_out.transpose(1, 0, 2), seq_out.T)


def solution(mesh):
    return jax.shard_map(
        local,
        mesh=mesh,
        in_specs=(P("row", "col", None), P(None, "col")) + (P(),) * 9,
        out_specs=(P("row", "col", None), P("row", "col")),
        check_vma=False,
    )
```

```python
import functools
import math

import jax
import jax.numpy as jnp
from jax import lax
from jax.experimental import pallas as pl
from jax.experimental.pallas import tpu as pltpu
from jax.sharding import PartitionSpec as P

HEADS = 32
LANES = 128
eps_norm = 1e-05
f32 = jnp.float32
bf16 = jnp.bfloat16


def layer_norm(values_in):
    row_mean = jnp.mean(values_in, axis=-1, keepdims=True)
    centred = values_in - row_mean
    row_var = jnp.mean(centred * centred, axis=-1, keepdims=True)
    return centred * lax.rsqrt(row_var + eps_norm)


def dot(a, b):
    return jnp.dot(a, b, preferred_element_type=f32)


def dot_nt(a, b):
    return lax.dot_general(a, b, (((1,), (1,)), ((), ())), preferred_element_type=f32)


def round_up(n, m):
    return -(-n // m) * m


def one_hot_rows(shape, target):
    rows = lax.broadcasted_iota(jnp.int32, shape, 0)
    cols = lax.broadcasted_iota(jnp.int32, shape, 1)
    return (cols == target(rows)).astype(f32).astype(bf16)


def call(kernel, outs, args, scratch=(), flops=1000, room=16):
    size = sum(a.size * a.dtype.itemsize for a, _ in args)
    size += sum(math.prod(a.shape) * jnp.dtype(a.dtype).itemsize for a in outs)
    space = {"V": pltpu.VMEM, "H": pltpu.HBM}
    return pl.pallas_call(
        kernel,
        out_shape=outs,
        in_specs=[pl.BlockSpec(memory_space=space[where]) for _, where in args],
        out_specs=tuple(pl.BlockSpec(memory_space=pltpu.VMEM) for _ in outs),
        scratch_shapes=list(scratch),
        compiler_params=pltpu.CompilerParams(vmem_limit_bytes=room * 1024 * 1024),
        cost_estimate=pl.CostEstimate(flops=flops, bytes_accessed=size, transcendentals=0),
    )(*[pltpu.with_memory_space_constraint(a, space[where]) for a, where in args])


def copies(sources, targets, sems):
    started = [
        pltpu.make_async_copy(s, t, sems.at[k]) for k, (s, t) in enumerate(zip(sources, targets))
    ]
    for one in started:
        one.start()
    return lambda k: started[k].wait()


def pack_seq(n_row, rows, seq_ref, msg_ref):
    feats = seq_ref.shape[0]
    fold = LANES // feats
    short = rows // fold
    row = lax.axis_index("row")
    for v in range(n_row):

        @pl.when(row == v)
        def _():
            parts = [
                seq_ref[:, v * rows + p * short : v * rows + (p + 1) * short].astype(f32)
                for p in range(fold)
            ]
            tile = jnp.concatenate(parts, axis=0).T.astype(bf16)
            msg_ref[:, :short, :] = jnp.broadcast_to(tile[None], (msg_ref.shape[0],) + tile.shape)


def bias_plan(rows, cols, n_col):
    own = rows // n_col
    keys = round_up(cols, 16)
    per_tile = LANES // HEADS
    full, rest = divmod(own, per_tile)
    split = per_tile // rest if rest and per_tile % rest == 0 else 1
    if rest and (keys // split) % 8:
        split = 1
    height = full * keys + (keys // split if rest else 0)
    return own, keys, full, rest, split, height


def prepare(n_row, n_col, chunk, *refs):
    mid_ref, msg_ref, seq_ref, hidden_ref, back_ref, bias_ref, pair_ref, norm_ref, sems = refs[5:]
    wait = copies(refs[:5], (seq_ref, hidden_ref, back_ref, bias_ref, pair_ref), sems)
    cols, rows, chans = pair_ref.shape
    short = rows * seq_ref.shape[0] // LANES
    wait(0)
    pack_seq(n_row, rows, seq_ref, msg_ref)
    for k in range(1, 5):
        wait(k)
    own, keys, full, rest, split, _ = bias_plan(rows, cols, n_col)
    per_tile = LANES // HEADS
    if keys > cols:
        norm_ref[cols * rows :, :] = jnp.zeros(((keys - cols) * rows, chans), f32)

    def step(t):
        at = t * chunk
        pair = pair_ref[pl.ds(at, chunk)].reshape(chunk * rows, chans).astype(f32)
        normed = layer_norm(pair).astype(bf16)
        hidden = jnp.maximum(dot(normed, hidden_ref[...]), 0.0).astype(bf16)
        mid = (pair + dot(hidden, back_ref[...])).astype(bf16)
        mid_ref[pl.ds(at, chunk)] = mid.reshape(chunk, rows, chans)
        start = at * rows if isinstance(at, int) else pl.multiple_of(at * rows, 8)
        norm_ref[pl.ds(start, chunk * rows), :] = layer_norm(mid.astype(f32))

    if cols // chunk <= 4:
        for t in range(cols // chunk):
            step(t)
    else:
        pl.loop(0, cols // chunk)(step)

    w_t = bias_ref[...]
    zero = jnp.zeros_like(w_t)
    placed = [
        jnp.concatenate([w_t if k == p else zero for k in range(per_tile)], axis=0)
        for p in range(per_tile)
    ]

    def queries(q):
        parts = [norm_ref[pl.ds(c * own + q, keys, stride=rows), :] for c in range(n_col)]
        return jnp.concatenate(parts, axis=0)

    for tile in range(full):
        wide = jnp.concatenate(
            [queries(tile * per_tile + p).astype(bf16) for p in range(per_tile)], axis=1
        )
        acc = dot_nt(wide, jnp.concatenate(placed, axis=1))
        at = short + tile * keys
        msg_ref[:, at : at + keys, :] = acc.reshape(n_col, keys, LANES).astype(bf16)
    if rest:
        small = keys // split
        lhs, rhs = [], []
        for p in range(rest):
            q_rows = queries(full * per_tile + p).reshape(n_col, split, small, chans)
            for s in range(split):
                lhs.append(q_rows[:, s].reshape(n_col * small, chans).astype(bf16))
                rhs.append(placed[s * rest + p])
        acc = dot_nt(jnp.concatenate(lhs, axis=1), jnp.concatenate(rhs, axis=1))
        msg_ref[:, short + full * keys :, :] = acc.reshape(n_col, small, LANES).astype(bf16)


def attend(n_row, plan, rows, cols, *refs):
    own, keys, full, rest, split, _ = plan
    n_in = 2 if n_row == 2 else 1
    seq_refs = refs[:n_in]
    wk_ref, *hbm_refs = refs[n_in : n_in + 5]
    out_ref, wq_ref, wv_ref, wo_ref, wp_ref, x_ref, xn_ref, k_ref, v_ref, bias_ref, sems = refs[
        n_in + 5 :
    ]
    wait = copies(hbm_refs, (wq_ref, wv_ref, wo_ref, wp_ref), sems)
    n_col = seq_refs[0].shape[-3]
    length, width = x_ref.shape
    feats = width // n_col
    fold = LANES // feats
    short = rows // fold
    head_dim = width // HEADS
    padded = round_up(own, 8)
    row, col = lax.axis_index("row"), lax.axis_index("col")
    slot = lax.broadcasted_iota(jnp.int32, (short, LANES), 1) // feats

    def place(read, v):
        for g in range(width // LANES):
            got = [read(fold * g + s).astype(f32) for s in range(fold)]
            for p in range(fold):
                piece = got[p]
                for s in range(fold):
                    if s != p:
                        piece = jnp.where(
                            slot == s, pltpu.roll(got[s], (s - p) % fold * feats, 1), piece
                        )
                start = pl.multiple_of(v * rows + p * short, 16)
                x_ref[pl.ds(start, short), g * LANES : (g + 1) * LANES] = piece

    if n_row == 2:
        place(lambda c: seq_refs[0][c, :short, :], row)
        place(lambda c: seq_refs[1][c, :short, :], 1 - row)
        bias_of = lambda c, at, size: seq_refs[0][c, short + at : short + at + size, :]
    else:
        pl.loop(0, n_row)(lambda v: place(lambda c: seq_refs[0][v, c, :short, :], v))
        bias_of = lambda c, at, size: seq_refs[0][row, c, short + at : short + at + size, :]

    block = rows * (2 if n_row == 2 else 1)

    def over_blocks(step):
        if length == block:
            step(pl.ds(0, block))
        else:
            pl.loop(0, length // block)(lambda b: step(pl.ds(pl.multiple_of(b * block, 16), block)))

    def norm_and_keys(at):
        normed = layer_norm(x_ref[at, :]).astype(bf16)
        xn_ref[at, :] = normed
        k_ref[at, :] = dot(normed, wk_ref[...]).astype(bf16)

    def values(at):
        v_ref[at, :] = dot(xn_ref[at, :], wv_ref[...]).astype(bf16)

    over_blocks(norm_and_keys)

    pick = one_hot_rows((padded, length), lambda i: row * rows + col * own + i)
    own_seq = dot(pick, x_ref[...].astype(bf16))
    own_norm = dot(pick, xn_ref[...]).astype(bf16)
    wait(0)
    queries = dot(own_norm, wq_ref[...]).astype(bf16)
    spread = one_hot_rows((padded * HEADS, padded), lambda ih: ih // HEADS)
    wide = dot(spread, queries)
    head_of_row = lax.broadcasted_iota(jnp.int32, wide.shape, 0) % HEADS
    head_of_lane = lax.broadcasted_iota(jnp.int32, wide.shape, 1) // head_dim
    same_head = head_of_row == head_of_lane
    by_head = jnp.where(same_head, wide, 0.0).astype(bf16)

    small = keys // split
    for c in range(n_col):
        for tile in range(full):
            bias_ref[c * cols : (c + 1) * cols, tile * LANES : (tile + 1) * LANES] = bias_of(
                c, tile * keys, keys
            ).astype(f32)[:cols]
        if rest:
            last = bias_of(c, full * keys, small).astype(f32)
            for s in range(split):
                height = min(small, cols - s * small)
                if height <= 0:
                    continue
                moved = last
                if s:
                    moved = pltpu.roll(last, LANES - s * rest * HEADS, 1)
                bias_ref[c * cols + s * small : c * cols + s * small + height, full * LANES :] = (
                    moved[:height]
                )
    scores = dot_nt(k_ref[...], by_head) * head_dim ** (-0.5) + bias_ref[...]
    top = jnp.max(scores, axis=0, keepdims=True)
    weights = jnp.exp(scores - top)
    denom = jnp.sum(weights, axis=0, keepdims=True)
    by_query = (weights / denom).T
    high = by_query.astype(bf16)
    low = (by_query - high.astype(f32)).astype(bf16)
    wait(1)
    over_blocks(values)
    mixed = dot(high, v_ref[...]) + dot(low, v_ref[...])
    mixed = jnp.where(same_head, mixed, 0.0)
    attended = jnp.sum(mixed.reshape(padded, HEADS, width), axis=1).astype(bf16)
    wait(2)
    seq_next = (own_seq + dot(attended, wo_ref[...])).astype(bf16)
    seq_wide = seq_next.astype(f32)
    wait(3)
    projected = dot(layer_norm(seq_wide).astype(bf16), wp_ref[...]).astype(bf16).astype(f32)
    for g in range(width // LANES):
        tile = jnp.concatenate([projected, seq_wide[:, g * LANES : (g + 1) * LANES]], axis=0)
        out_ref[:, fold * g : fold * (g + 1)] = jnp.broadcast_to(
            tile.astype(bf16)[None, None], (n_row, fold) + tile.shape
        )


def update_pair(own, fold, msg_ref, mid_ref, wpair_ref, pair_ref, seq_ref, left_ref, slab_ref):
    cols, rows, chans = mid_ref.shape
    n_row, n_col, twice, _ = msg_ref.shape
    padded = twice // 2
    half = chans // 2
    row, col = lax.axis_index("row"), lax.axis_index("col")
    for c in range(n_col):
        block = msg_ref[row, c].astype(f32)
        left_ref[c * own : (c + 1) * own, :] = block[:own]
        slab_ref[c * own : (c + 1) * own, :] = block[padded : padded + own]
    feats = LANES // fold
    turned = slab_ref[...].T
    for s in range(fold):

        @pl.when(lax.rem(col, fold) == s)
        def _():
            seq_ref[...] = turned[s * feats : (s + 1) * feats].astype(bf16)

    both = left_ref[...]
    is_first = lax.broadcasted_iota(jnp.int32, (1, chans), 1) < half
    left = jnp.where(is_first, both, pltpu.roll(both, half, 1))
    blocks_each = cols // own
    first = col * blocks_each

    def step(t):
        at = first + t
        theirs = msg_ref[at // n_col, lax.rem(at, n_col)].astype(f32)[:padded]
        right = jnp.where(is_first, pltpu.roll(theirs, half, 1), theirs)
        feature = []
        for i in range(own):
            r = right[i : i + 1]
            feature.append(jnp.where(is_first, left * r, left - r).astype(bf16))
        out = dot(jnp.concatenate(feature, axis=0), wpair_ref[...])
        here = pl.ds(t * own, own)
        mid = mid_ref[here].astype(f32)
        pair_ref[here] = (mid + out.reshape(own, rows, chans)).astype(bf16)

    if blocks_each <= 4:
        for t in range(blocks_each):
            step(t)
    else:
        pl.loop(0, blocks_each)(step)


def local(pair, seq, w_hidden, w_back, w_bias, w_query, w_key, w_value, w_out, w_project, w_pair):
    shape = pltpu.VMEM
    rows, cols, chans = pair.shape
    length, feats = seq.shape
    width = w_query.shape[0]
    n_row, n_col = lax.axis_size("row"), lax.axis_size("col")
    fold = LANES // feats
    short = rows // fold
    plan = bias_plan(rows, cols, n_col)
    own, keys, full, rest, _, height = plan
    padded = round_up(own, 8)
    hidden_units = w_hidden.shape[1]

    chunk = max(k for k in range(1, cols + 1) if cols % k == 0 and k * rows <= 576)
    pair_mid, msg = call(
        functools.partial(prepare, n_row, n_col, chunk),
        (shape((cols, rows, chans), bf16), shape((n_col, short + height, LANES), bf16)),
        [(a, "H") for a in (seq.T, w_hidden, w_back, w_bias.T, pair.transpose(1, 0, 2))],
        [
            shape((feats, length), bf16),
            shape(w_hidden.shape, bf16),
            shape(w_back.shape, bf16),
            shape(w_bias.shape[::-1], bf16),
            shape((cols, rows, chans), bf16),
            shape((keys * rows, chans), f32),
            pltpu.SemaphoreType.DMA((5,)),
        ],
        flops=4 * rows * cols * chans * hidden_units,
        room=24,
    )
    got = lax.all_to_all(msg, "col", split_axis=0, concat_axis=0, tiled=True)
    if n_row == 2:
        parts = (got, lax.ppermute(got, "row", [(0, 1), (1, 0)]))
    else:
        parts = (lax.all_gather(got, "row"),)
    (out_msg,) = call(
        functools.partial(attend, n_row, plan, rows, cols),
        (shape((n_row, n_col, 2 * padded, LANES), bf16),),
        [(a, "V") for a in parts + (w_key,)]
        + [(a, "H") for a in (w_query, w_value, w_out, w_project)],
        [
            shape((width, width), bf16),
            shape((width, width), bf16),
            shape((width, width), bf16),
            shape(w_project.shape, bf16),
            shape((length, width), f32),
            shape((length, width), bf16),
            shape((length, width), bf16),
            shape((length, width), bf16),
            shape((length, padded * HEADS), f32),
            pltpu.SemaphoreType.DMA((4,)),
        ],
        flops=6 * length * width * width,
        room=40,
    )
    flat = out_msg.reshape(n_row * n_col, 2 * padded, LANES)
    got = lax.all_to_all(flat, ("row", "col"), split_axis=0, concat_axis=0, tiled=True)
    pair_out, seq_out = call(
        functools.partial(update_pair, own, fold),
        (
            jax.ShapeDtypeStruct((cols, rows, chans), bf16),
            jax.ShapeDtypeStruct((feats, rows), bf16),
        ),
        [(a, "V") for a in (got.reshape(out_msg.shape), pair_mid, w_pair)],
        [pltpu.VMEM((rows, LANES), f32), pltpu.VMEM((rows, LANES), f32)],
        flops=2 * rows * cols * chans * chans,
    )
    return (pair_out.transpose(1, 0, 2), seq_out.T)


def solution(mesh):
    return jax.shard_map(
        local,
        mesh=mesh,
        in_specs=(P("row", "col", None), P(None, "col")) + (P(),) * 9,
        out_specs=(P("row", "col", None), P("row", "col")),
        check_vma=False,
    )
```

```python
import functools
import math

import jax
import jax.numpy as jnp
from jax import lax
from jax.experimental import pallas as pl
from jax.experimental.pallas import tpu as pltpu
from jax.sharding import PartitionSpec as P

HEADS = 32
LANES = 128
eps_norm = 1e-05
f32 = jnp.float32
bf16 = jnp.bfloat16


def layer_norm(values_in):
    row_mean = jnp.mean(values_in, axis=-1, keepdims=True)
    centred = values_in - row_mean
    row_var = jnp.mean(centred * centred, axis=-1, keepdims=True)
    return centred * lax.rsqrt(row_var + eps_norm)


def dot(a, b):
    return jnp.dot(a, b, preferred_element_type=f32)


def dot_nt(a, b):
    return lax.dot_general(a, b, (((1,), (1,)), ((), ())), preferred_element_type=f32)


def round_up(n, m):
    return -(-n // m) * m


def one_hot_rows(shape, target):
    rows = lax.broadcasted_iota(jnp.int32, shape, 0)
    cols = lax.broadcasted_iota(jnp.int32, shape, 1)
    return (cols == target(rows)).astype(f32).astype(bf16)


def call(kernel, outs, args, scratch=(), flops=1000, room=16):
    size = sum(a.size * a.dtype.itemsize for a, _ in args)
    size += sum(math.prod(a.shape) * jnp.dtype(a.dtype).itemsize for a in outs)
    space = {"V": pltpu.VMEM, "H": pltpu.HBM}
    return pl.pallas_call(
        kernel,
        out_shape=outs,
        in_specs=[pl.BlockSpec(memory_space=space[where]) for _, where in args],
        out_specs=tuple(pl.BlockSpec(memory_space=pltpu.VMEM) for _ in outs),
        scratch_shapes=list(scratch),
        compiler_params=pltpu.CompilerParams(vmem_limit_bytes=room * 1024 * 1024),
        cost_estimate=pl.CostEstimate(flops=flops, bytes_accessed=size, transcendentals=0),
    )(*[pltpu.with_memory_space_constraint(a, space[where]) for a, where in args])


def copies(sources, targets, sems):
    started = [
        pltpu.make_async_copy(s, t, sems.at[k]) for k, (s, t) in enumerate(zip(sources, targets))
    ]
    for one in started:
        one.start()
    return lambda k: started[k].wait()


def stage(body):
    pl.when(lax.axis_index("row") >= 0)(body)


def pack_seq(n_row, rows, seq_ref, msg_ref):
    feats = seq_ref.shape[0]
    fold = LANES // feats
    short = rows // fold
    row = lax.axis_index("row")
    for v in range(n_row):

        @pl.when(row == v)
        def _():
            parts = [
                seq_ref[:, v * rows + p * short : v * rows + (p + 1) * short].astype(f32)
                for p in range(fold)
            ]
            tile = jnp.concatenate(parts, axis=0).T.astype(bf16)
            msg_ref[:, :short, :] = jnp.broadcast_to(tile[None], (msg_ref.shape[0],) + tile.shape)


def bias_plan(rows, cols, n_col):
    own = rows // n_col
    keys = round_up(cols, 16)
    per_tile = LANES // HEADS
    full, rest = divmod(own, per_tile)
    split = per_tile // rest if rest and per_tile % rest == 0 else 1
    if rest and (keys // split) % 8:
        split = 1
    height = full * keys + (keys // split if rest else 0)
    return own, keys, full, rest, split, height


def prepare(n_row, n_col, chunk, *refs):
    mid_ref, msg_ref, wk_ref, seq_ref, hidden_ref, back_ref, bias_ref, pair_ref, norm_ref, sems = (
        refs[6:]
    )
    wait = copies(refs[:6], (seq_ref, hidden_ref, back_ref, bias_ref, pair_ref, wk_ref), sems)
    cols, rows, chans = pair_ref.shape
    short = rows * seq_ref.shape[0] // LANES
    wait(0)
    pack_seq(n_row, rows, seq_ref, msg_ref)
    for k in range(1, 5):
        wait(k)
    stage(lambda: transition(n_row, n_col, chunk, short, hidden_ref, back_ref, bias_ref, pair_ref, mid_ref, msg_ref, norm_ref))
    wait(5)


def transition(
    n_row, n_col, chunk, short, hidden_ref, back_ref, bias_ref, pair_ref, mid_ref, msg_ref, norm_ref
):
    cols, rows, chans = pair_ref.shape
    own, keys, full, rest, split, _ = bias_plan(rows, cols, n_col)
    per_tile = LANES // HEADS
    if keys > cols:
        norm_ref[cols * rows :, :] = jnp.zeros(((keys - cols) * rows, chans), f32)

    def step(t):
        at = t * chunk
        pair = pair_ref[pl.ds(at, chunk)].reshape(chunk * rows, chans).astype(f32)
        normed = layer_norm(pair).astype(bf16)
        hidden = jnp.maximum(dot(normed, hidden_ref[...]), 0.0).astype(bf16)
        mid = (pair + dot(hidden, back_ref[...])).astype(bf16)
        mid_ref[pl.ds(at, chunk)] = mid.reshape(chunk, rows, chans)
        start = at * rows if isinstance(at, int) else pl.multiple_of(at * rows, 8)
        norm_ref[pl.ds(start, chunk * rows), :] = layer_norm(mid.astype(f32))

    if cols // chunk <= 4:
        for t in range(cols // chunk):
            step(t)
    else:
        pl.loop(0, cols // chunk)(step)

    w_t = bias_ref[...]
    zero = jnp.zeros_like(w_t)
    placed = [
        jnp.concatenate([w_t if k == p else zero for k in range(per_tile)], axis=0)
        for p in range(per_tile)
    ]

    def queries(q):
        parts = [norm_ref[pl.ds(c * own + q, keys, stride=rows), :] for c in range(n_col)]
        return jnp.concatenate(parts, axis=0)

    for tile in range(full):
        wide = jnp.concatenate(
            [queries(tile * per_tile + p).astype(bf16) for p in range(per_tile)], axis=1
        )
        acc = dot_nt(wide, jnp.concatenate(placed, axis=1))
        at = short + tile * keys
        msg_ref[:, at : at + keys, :] = acc.reshape(n_col, keys, LANES).astype(bf16)
    if rest:
        small = keys // split
        lhs, rhs = [], []
        for p in range(rest):
            q_rows = queries(full * per_tile + p).reshape(n_col, split, small, chans)
            for s in range(split):
                lhs.append(q_rows[:, s].reshape(n_col * small, chans).astype(bf16))
                rhs.append(placed[s * rest + p])
        acc = dot_nt(jnp.concatenate(lhs, axis=1), jnp.concatenate(rhs, axis=1))
        msg_ref[:, short + full * keys :, :] = acc.reshape(n_col, small, LANES).astype(bf16)


def place(read, feats, short, x_ref, start):
    fold = LANES // feats
    slot = lax.broadcasted_iota(jnp.int32, (short, LANES), 1) // feats
    for g in range(x_ref.shape[1] // LANES):
        got = [read(fold * g + s).astype(f32) for s in range(fold)]
        for p in range(fold):
            piece = got[p]
            for s in range(fold):
                if s != p:
                    piece = jnp.where(
                        slot == s, pltpu.roll(got[s], (s - p) % fold * feats, 1), piece
                    )
            at = pl.multiple_of(start + p * short, 16)
            x_ref[pl.ds(at, short), g * LANES : (g + 1) * LANES] = piece


def own_block(
    plan, rows, cols,
    got_ref, wk_ref, wq_hbm,
    x_out, k_ref, by_head_ref, own_ref, bias_ref,
    wq_ref, x_ref, raw_ref, norm_ref, sems,
):
    wait = copies((wq_hbm,), (wq_ref,), sems)
    own, keys, full, rest, split, _ = plan
    n_col = got_ref.shape[0]
    width = x_ref.shape[1]
    feats = width // n_col
    short = rows * feats // LANES
    head_dim = width // HEADS
    padded = own_ref.shape[0]
    col = lax.axis_index("col")
    @stage
    def _():
        place(lambda c: got_ref[c, :short, :], feats, short, x_ref, 0)
        normed = layer_norm(x_ref[...]).astype(bf16)
        x_out[...] = normed
        pick = one_hot_rows((padded, rows), lambda i: col * own + i)
        own_ref[...] = dot(pick, x_ref[...].astype(bf16))
        norm_ref[...] = dot(pick, normed).astype(bf16)
        k_ref[...] = dot(normed, wk_ref[...]).astype(bf16)

        small = keys // split
        for c in range(n_col):
            for tile in range(full):
                at = short + tile * keys
                raw_ref[c * cols : (c + 1) * cols, tile * LANES : (tile + 1) * LANES] = got_ref[
                    c, at : at + keys, :
                ].astype(f32)[:cols]
            if rest:
                last = got_ref[c, short + full * keys : short + full * keys + small, :].astype(f32)
                for s in range(split):
                    height = min(small, cols - s * small)
                    if height <= 0:
                        continue
                    moved = last
                    if s:
                        moved = pltpu.roll(last, LANES - s * rest * HEADS, 1)
                    raw_ref[c * cols + s * small : c * cols + s * small + height, full * LANES :] = (
                        moved[:height]
                    )
        given = (raw_ref.shape[1], padded * HEADS)
        source = lax.broadcasted_iota(jnp.int32, given, 0)
        target = lax.broadcasted_iota(jnp.int32, given, 1)
        query = target % padded
        same = (source == query * HEADS + target // padded) & (query < own)
        bias_ref[...] = dot(raw_ref[...].astype(bf16), same.astype(f32).astype(bf16))

    wait(0)

    @stage
    def _():
        queries = dot(norm_ref[...], wq_ref[...]).astype(bf16)
        spread = one_hot_rows((padded * HEADS, padded), lambda hi: hi % padded)
        wide = dot(spread, queries)
        head_of_row = lax.broadcasted_iota(jnp.int32, wide.shape, 0) // padded
        head_of_lane = lax.broadcasted_iota(jnp.int32, wide.shape, 1) // head_dim
        by_head_ref[...] = jnp.where(head_of_row == head_of_lane, wide, 0.0).astype(bf16)


def attend(
    rows,
    others_ref, x_own, k_own, by_head_ref, own_ref, bias_ref, wk_ref, wv_hbm, wo_hbm, wp_hbm,
    out_ref,
    wv_ref, wo_ref, wp_ref, x_ref, xn_ref, k_ref, v_ref, w_ref, att_ref, sems,
):
    wait = copies((wv_hbm, wo_hbm, wp_hbm), (wv_ref, wo_ref, wp_ref), sems)
    n_col = others_ref.shape[-3]
    n_row = out_ref.shape[0]
    length, width = k_ref.shape
    feats = width // n_col
    fold = LANES // feats
    short = rows // fold
    head_dim = width // HEADS
    padded = own_ref.shape[0]
    row = lax.axis_index("row")

    def block(read, v):
        place(read, feats, short, x_ref, 0)
        normed = layer_norm(x_ref[...]).astype(bf16)
        at = pl.ds(pl.multiple_of(v * rows, 16), rows)
        xn_ref[at, :] = normed
        k_ref[at, :] = dot(normed, wk_ref[...]).astype(bf16)

    @stage
    def _():
        if n_row == 2:
            block(lambda c: others_ref[c, :short, :], 1 - row)
        else:
            pl.loop(0, n_row)(lambda v: block(lambda c: others_ref[v, c, :short, :], v))
        mine = pl.ds(pl.multiple_of(row * rows, 16), rows)
        xn_ref[mine, :] = x_own[...]
        k_ref[mine, :] = k_own[...]
        scores = dot_nt(k_ref[...], by_head_ref[...]) * head_dim ** (-0.5) + bias_ref[...]
        top = jnp.max(scores, axis=0, keepdims=True)
        weights = jnp.exp(scores - top)
        denom = jnp.sum(weights, axis=0, keepdims=True)
        w_ref[...] = (weights / denom).T

    wait(0)
    step = rows * (2 if n_row == 2 else 1)
    per_group = LANES // head_dim
    tall = per_group * padded

    @stage
    def _():
        if length == step:
            v_ref[...] = dot(xn_ref[...], wv_ref[...]).astype(bf16)
        else:

            @pl.loop(0, length // step)
            def _(b):
                at = pl.ds(pl.multiple_of(b * step, 16), step)
                v_ref[at, :] = dot(xn_ref[at, :], wv_ref[...]).astype(bf16)

        lane_head = lax.broadcasted_iota(jnp.int32, (padded, LANES), 1) // head_dim
        groups = []
        for g in range(width // LANES):
            weights = w_ref[g * tall : (g + 1) * tall, :]
            high = weights.astype(bf16)
            low = (weights - high.astype(f32)).astype(bf16)
            both = jnp.concatenate([high, low], axis=0)
            mixed = dot(both, v_ref[:, g * LANES : (g + 1) * LANES])
            mixed = mixed[:tall] + mixed[tall:]
            chosen = mixed[:padded]
            for h in range(1, per_group):
                chosen = jnp.where(lane_head == h, mixed[h * padded : (h + 1) * padded], chosen)
            groups.append(chosen)
        att_ref[...] = jnp.concatenate(groups, axis=1).astype(bf16)

    wait(1)
    wait(2)

    @stage
    def _():
        seq_next = (own_ref[...] + dot(att_ref[...], wo_ref[...])).astype(bf16)
        seq_wide = seq_next.astype(f32)
        projected = dot(layer_norm(seq_wide).astype(bf16), wp_ref[...]).astype(bf16).astype(f32)
        for g in range(width // LANES):
            tile = jnp.concatenate([projected, seq_wide[:, g * LANES : (g + 1) * LANES]], axis=0)
            out_ref[:, fold * g : fold * (g + 1)] = jnp.broadcast_to(
                tile.astype(bf16)[None, None], (n_row, fold) + tile.shape
            )


def update_pair(own, fold, msg_ref, mid_ref, wpair_ref, pair_ref, seq_ref, left_ref, slab_ref):
    cols, rows, chans = mid_ref.shape
    n_row, n_col, twice, _ = msg_ref.shape
    padded = twice // 2
    half = chans // 2
    row, col = lax.axis_index("row"), lax.axis_index("col")
    for c in range(n_col):
        block = msg_ref[row, c].astype(f32)
        left_ref[c * own : (c + 1) * own, :] = block[:own]
        slab_ref[c * own : (c + 1) * own, :] = block[padded : padded + own]
    feats = LANES // fold
    turned = slab_ref[...].T
    for s in range(fold):

        @pl.when(lax.rem(col, fold) == s)
        def _():
            seq_ref[...] = turned[s * feats : (s + 1) * feats].astype(bf16)

    both = left_ref[...]
    is_first = lax.broadcasted_iota(jnp.int32, (1, chans), 1) < half
    left = jnp.where(is_first, both, pltpu.roll(both, half, 1))
    blocks_each = cols // own
    first = col * blocks_each

    def step(t):
        at = first + t
        theirs = msg_ref[at // n_col, lax.rem(at, n_col)].astype(f32)[:padded]
        right = jnp.where(is_first, pltpu.roll(theirs, half, 1), theirs)
        feature = []
        for i in range(own):
            r = right[i : i + 1]
            feature.append(jnp.where(is_first, left * r, left - r).astype(bf16))
        out = dot(jnp.concatenate(feature, axis=0), wpair_ref[...])
        here = pl.ds(t * own, own)
        mid = mid_ref[here].astype(f32)
        pair_ref[here] = (mid + out.reshape(own, rows, chans)).astype(bf16)

    if blocks_each <= 4:
        for t in range(blocks_each):
            step(t)
    else:
        pl.loop(0, blocks_each)(step)


def local(pair, seq, w_hidden, w_back, w_bias, w_query, w_key, w_value, w_out, w_project, w_pair):
    shape = pltpu.VMEM
    rows, cols, chans = pair.shape
    length, feats = seq.shape
    width = w_query.shape[0]
    n_row, n_col = lax.axis_size("row"), lax.axis_size("col")
    fold = LANES // feats
    short = rows // fold
    plan = bias_plan(rows, cols, n_col)
    own, keys, full, rest, _, height = plan
    padded = round_up(own, 8)
    hidden_units = w_hidden.shape[1]

    chunk = max(k for k in range(1, cols + 1) if cols % k == 0 and k * rows <= 576)
    pair_mid, msg, wk = call(
        functools.partial(prepare, n_row, n_col, chunk),
        (
            shape((cols, rows, chans), bf16),
            shape((n_col, short + height, LANES), bf16),
            shape((width, width), bf16),
        ),
        [(a, "H") for a in (seq.T, w_hidden, w_back, w_bias.T, pair.transpose(1, 0, 2), w_key)],
        [
            shape((feats, length), bf16),
            shape(w_hidden.shape, bf16),
            shape(w_back.shape, bf16),
            shape(w_bias.shape[::-1], bf16),
            shape((cols, rows, chans), bf16),
            shape((keys * rows, chans), f32),
            pltpu.SemaphoreType.DMA((6,)),
        ],
        flops=4 * rows * cols * chans * hidden_units,
        room=24,
    )
    got = lax.all_to_all(msg, "col", split_axis=0, concat_axis=0, tiled=True)
    if n_row == 2:
        others = lax.ppermute(got, "row", [(0, 1), (1, 0)])
    else:
        others = lax.all_gather(got, "row")
    tiles = full + (1 if rest else 0)
    x_own, k_own, by_head, own_seq, bias = call(
        functools.partial(own_block, plan, rows, cols),
        (
            shape((rows, width), bf16),
            shape((rows, width), bf16),
            shape((padded * HEADS, width), bf16),
            shape((padded, width), f32),
            shape((length, padded * HEADS), f32),
        ),
        [(got, "V"), (wk, "V"), (w_query, "H")],
        [
            shape((width, width), bf16),
            shape((rows, width), f32),
            shape((length, tiles * LANES), f32),
            shape((padded, width), bf16),
            pltpu.SemaphoreType.DMA((1,)),
        ],
        flops=6 * rows * width * width,
        room=16,
    )
    (out_msg,) = call(
        functools.partial(attend, rows),
        (shape((n_row, n_col, 2 * padded, LANES), bf16),),
        [(a, "V") for a in (others, x_own, k_own, by_head, own_seq, bias, wk)]
        + [(a, "H") for a in (w_value, w_out, w_project)],
        [
            shape((width, width), bf16),
            shape((width, width), bf16),
            shape(w_project.shape, bf16),
            shape((rows, width), f32),
            shape((length, width), bf16),
            shape((length, width), bf16),
            shape((length, width), bf16),
            shape((padded * HEADS, length), f32),
            shape((padded, width), bf16),
            pltpu.SemaphoreType.DMA((3,)),
        ],
        flops=6 * length * width * width,
        room=32,
    )
    flat = out_msg.reshape(n_row * n_col, 2 * padded, LANES)
    got = lax.all_to_all(flat, ("row", "col"), split_axis=0, concat_axis=0, tiled=True)
    pair_out, seq_out = call(
        functools.partial(update_pair, own, fold),
        (
            jax.ShapeDtypeStruct((cols, rows, chans), bf16),
            jax.ShapeDtypeStruct((feats, rows), bf16),
        ),
        [(a, "V") for a in (got.reshape(out_msg.shape), pair_mid, w_pair)],
        [pltpu.VMEM((rows, LANES), f32), pltpu.VMEM((rows, LANES), f32)],
        flops=2 * rows * cols * chans * chans,
    )
    return (pair_out.transpose(1, 0, 2), seq_out.T)


def solution(mesh):
    return jax.shard_map(
        local,
        mesh=mesh,
        in_specs=(P("row", "col", None), P(None, "col")) + (P(),) * 9,
        out_specs=(P("row", "col", None), P("row", "col")),
        check_vma=False,
    )
```

```python
import functools
import math

import jax
import jax.numpy as jnp
from jax import lax
from jax.experimental import pallas as pl
from jax.experimental.pallas import tpu as pltpu
from jax.sharding import PartitionSpec as P

HEADS = 32
LANES = 128
eps_norm = 1e-05
f32 = jnp.float32
bf16 = jnp.bfloat16


def layer_norm(values_in):
    row_mean = jnp.mean(values_in, axis=-1, keepdims=True)
    centred = values_in - row_mean
    row_var = jnp.mean(centred * centred, axis=-1, keepdims=True)
    return centred * lax.rsqrt(row_var + eps_norm)


def dot(a, b):
    return jnp.dot(a, b, preferred_element_type=f32)


def dot_nt(a, b):
    return lax.dot_general(a, b, (((1,), (1,)), ((), ())), preferred_element_type=f32)


def round_up(n, m):
    return -(-n // m) * m


def one_hot_rows(shape, target):
    rows = lax.broadcasted_iota(jnp.int32, shape, 0)
    cols = lax.broadcasted_iota(jnp.int32, shape, 1)
    return (cols == target(rows)).astype(f32).astype(bf16)


def call(kernel, outs, args, scratch=(), flops=1000, room=16):
    size = sum(a.size * a.dtype.itemsize for a, _ in args)
    size += sum(math.prod(a.shape) * jnp.dtype(a.dtype).itemsize for a in outs)
    space = {"V": pltpu.VMEM, "H": pltpu.HBM}
    return pl.pallas_call(
        kernel,
        out_shape=outs,
        in_specs=[pl.BlockSpec(memory_space=space[where]) for _, where in args],
        out_specs=tuple(pl.BlockSpec(memory_space=pltpu.VMEM) for _ in outs),
        scratch_shapes=list(scratch),
        compiler_params=pltpu.CompilerParams(vmem_limit_bytes=room * 1024 * 1024),
        cost_estimate=pl.CostEstimate(flops=flops, bytes_accessed=size, transcendentals=0),
    )(*[pltpu.with_memory_space_constraint(a, space[where]) for a, where in args])


def copies(sources, targets, sems):
    started = [
        pltpu.make_async_copy(s, t, sems.at[k]) for k, (s, t) in enumerate(zip(sources, targets))
    ]
    for one in started:
        one.start()
    return lambda k: started[k].wait()


def stage(body):
    pl.when(lax.axis_index("row") >= 0)(body)


def pack_seq(n_row, rows, seq_ref, msg_ref):
    feats = seq_ref.shape[0]
    fold = LANES // feats
    short = rows // fold
    row = lax.axis_index("row")
    for v in range(n_row):

        @pl.when(row == v)
        def _():
            parts = [
                seq_ref[:, v * rows + p * short : v * rows + (p + 1) * short].astype(f32)
                for p in range(fold)
            ]
            tile = jnp.concatenate(parts, axis=0).T.astype(bf16)
            msg_ref[:, :short, :] = jnp.broadcast_to(tile[None], (msg_ref.shape[0],) + tile.shape)


def bias_plan(rows, cols, n_col):
    own = rows // n_col
    keys = round_up(cols, 16)
    per_tile = LANES // HEADS
    full, rest = divmod(own, per_tile)
    split = per_tile // rest if rest and per_tile % rest == 0 else 1
    if rest and (keys // split) % 8:
        split = 1
    height = full * keys + (keys // split if rest else 0)
    return own, keys, full, rest, split, height


def prepare(n_row, n_col, chunk, *refs):
    mid_ref, msg_ref, wq_ref, seq_ref, hidden_ref, back_ref, bias_ref, pair_ref = refs[6:14]
    *inner_refs, sems = refs[14:]
    wait = copies(refs[:6], (seq_ref, hidden_ref, back_ref, bias_ref, pair_ref, wq_ref), sems)
    cols, rows, chans = pair_ref.shape
    short = rows * seq_ref.shape[0] // LANES
    wait(0)
    pack_seq(n_row, rows, seq_ref, msg_ref)
    for k in range(1, 5):
        wait(k)

    @stage
    def _():
        weights = (hidden_ref, back_ref, bias_ref)
        transition(n_col, chunk, short, *weights, pair_ref, mid_ref, msg_ref, *inner_refs)

    wait(5)


def transition(
    n_col, chunk, short,
    hidden_ref, back_ref, bias_ref, pair_ref, mid_ref, msg_ref, norm_ref, full_ref, rest_ref,
):
    cols, rows, chans = pair_ref.shape
    own, keys, full, rest, split, _ = bias_plan(rows, cols, n_col)
    per_tile = LANES // HEADS
    def step(t):
        at = t * chunk
        pair = pair_ref[pl.ds(at, chunk)].reshape(chunk * rows, chans).astype(f32)
        normed = layer_norm(pair).astype(bf16)
        hidden = jnp.maximum(dot(normed, hidden_ref[...]), 0.0).astype(bf16)
        mid = (pair + dot(hidden, back_ref[...])).astype(bf16)
        mid_ref[pl.ds(at, chunk)] = mid.reshape(chunk, rows, chans)
        normed = layer_norm(mid.astype(f32)).astype(bf16)
        norm_ref[pl.ds(at, chunk)] = normed.reshape(chunk, rows, chans)

    if cols // chunk <= 4:
        for t in range(cols // chunk):
            step(t)
    else:
        pl.loop(0, cols // chunk)(step)

    w_t = bias_ref[...]
    zero = jnp.zeros_like(w_t)
    placed = [
        jnp.concatenate([w_t if k == p else zero for k in range(per_tile)], axis=0)
        for p in range(per_tile)
    ]

    def queries(q, first, last):
        some = norm_ref[first:last, q * n_col : (q + 1) * n_col, :]
        return some.reshape((last - first) * n_col, chans)

    def wide(qs, first, last):
        return jnp.concatenate([queries(q, first, last) for q in qs], axis=1)

    for tile in range(full):
        qs = range(tile * per_tile, (tile + 1) * per_tile)
        acc = dot_nt(wide(qs, 0, cols), jnp.concatenate(placed, axis=1))
        full_ref[tile, : cols * n_col, :] = acc
        if keys > cols:
            full_ref[tile, cols * n_col :, :] = jnp.zeros(((keys - cols) * n_col, LANES), f32)
    small = keys // split
    if rest:
        qs = range(full * per_tile, own)
        for s in range(split):
            first, last = s * small, min(cols, (s + 1) * small)
            if last <= first:
                continue
            acc = dot_nt(
                wide(qs, first, last),
                jnp.concatenate(placed[s * rest : (s + 1) * rest], axis=1),
            )
            if s:
                rest_ref[: (last - first) * n_col, :] += acc
            else:
                rest_ref[: (last - first) * n_col, :] = acc
    for c in range(n_col):
        parts = [full_ref[tile, pl.ds(c, keys, stride=n_col), :] for tile in range(full)]
        if rest:
            parts.append(rest_ref[pl.ds(c, small, stride=n_col), :])
        msg_ref[c, short:, :] = jnp.concatenate(parts, axis=0).astype(bf16)


def place(read, feats, short, x_ref, start):
    fold = LANES // feats
    slot = lax.broadcasted_iota(jnp.int32, (short, LANES), 1) // feats
    for g in range(x_ref.shape[1] // LANES):
        got = [read(fold * g + s).astype(f32) for s in range(fold)]
        for p in range(fold):
            piece = got[p]
            for s in range(fold):
                if s != p:
                    piece = jnp.where(
                        slot == s, pltpu.roll(got[s], (s - p) % fold * feats, 1), piece
                    )
            at = pl.multiple_of(start + p * short, 16)
            x_ref[pl.ds(at, short), g * LANES : (g + 1) * LANES] = piece


def own_block(
    plan, rows, cols,
    got_ref, wq_ref, wk_hbm,
    x_out, by_head_ref, own_ref, bias_ref, wk_ref,
    x_ref, raw_ref, sems,
):
    wait = copies((wk_hbm,), (wk_ref,), sems)
    own, keys, full, rest, split, _ = plan
    n_col = got_ref.shape[0]
    width = x_ref.shape[1]
    feats = width // n_col
    short = rows * feats // LANES
    head_dim = width // HEADS
    padded = own_ref.shape[0]
    col = lax.axis_index("col")
    @stage
    def _():
        place(lambda c: got_ref[c, :short, :], feats, short, x_ref, 0)
        normed = layer_norm(x_ref[...]).astype(bf16)
        x_out[...] = normed
        pick = one_hot_rows((padded, rows), lambda i: i * n_col + col)
        own_ref[...] = dot(pick, x_ref[...].astype(bf16))
        own_norm = dot(pick, normed).astype(bf16)

        small = keys // split
        for c in range(n_col):
            for tile in range(full):
                at = short + tile * keys
                raw_ref[c * cols : (c + 1) * cols, tile * LANES : (tile + 1) * LANES] = got_ref[
                    c, at : at + keys, :
                ].astype(f32)[:cols]
            if rest:
                last = got_ref[c, short + full * keys : short + full * keys + small, :].astype(f32)
                for s in range(split):
                    height = min(small, cols - s * small)
                    if height <= 0:
                        continue
                    moved = last
                    if s:
                        moved = pltpu.roll(last, LANES - s * rest * HEADS, 1)
                    raw_ref[c * cols + s * small : c * cols + s * small + height, full * LANES :] = (
                        moved[:height]
                    )
        given = (raw_ref.shape[1], padded * HEADS)
        source = lax.broadcasted_iota(jnp.int32, given, 0)
        target = lax.broadcasted_iota(jnp.int32, given, 1)
        query = target % padded
        same = (source == query * HEADS + target // padded) & (query < own)
        bias_ref[...] = dot(raw_ref[...].astype(bf16), same.astype(f32).astype(bf16))

        queries = dot(own_norm, wq_ref[...]).astype(bf16)
        spread = one_hot_rows((padded * HEADS, padded), lambda hi: hi % padded)
        wide = dot(spread, queries)
        head_of_row = lax.broadcasted_iota(jnp.int32, wide.shape, 0) // padded
        head_of_lane = lax.broadcasted_iota(jnp.int32, wide.shape, 1) // head_dim
        by_head_ref[...] = jnp.where(head_of_row == head_of_lane, wide, 0.0).astype(bf16)

    wait(0)


def attend(
    rows,
    others_ref, x_own, by_head_ref, own_ref, bias_ref, wk_ref, wv_hbm, wo_hbm, wp_hbm,
    out_ref,
    wv_ref, wo_ref, wp_ref, x_ref, xn_ref, k_ref, v_ref, w_ref, att_ref, sems,
):
    wait = copies((wv_hbm, wo_hbm, wp_hbm), (wv_ref, wo_ref, wp_ref), sems)
    n_col = others_ref.shape[-3]
    n_row = out_ref.shape[0]
    length, width = k_ref.shape
    feats = width // n_col
    fold = LANES // feats
    short = rows // fold
    head_dim = width // HEADS
    padded = own_ref.shape[0]
    row = lax.axis_index("row")

    def block(read, v):
        place(read, feats, short, x_ref, 0)
        normed = layer_norm(x_ref[...]).astype(bf16)
        at = pl.ds(pl.multiple_of(v * rows, 16), rows)
        xn_ref[at, :] = normed

    step = rows * (2 if n_row == 2 else 1)

    def project(w_of, out):
        if length == step:
            out[...] = dot(xn_ref[...], w_of[...]).astype(bf16)
        else:

            @pl.loop(0, length // step)
            def _(b):
                at = pl.ds(pl.multiple_of(b * step, 16), step)
                out[at, :] = dot(xn_ref[at, :], w_of[...]).astype(bf16)

    @stage
    def _():
        if n_row == 2:
            block(lambda c: others_ref[c, :short, :], 1 - row)
        else:
            pl.loop(0, n_row)(lambda v: block(lambda c: others_ref[v, c, :short, :], v))
        mine = pl.ds(pl.multiple_of(row * rows, 16), rows)
        xn_ref[mine, :] = x_own[...]
        project(wk_ref, k_ref)
        scores = dot_nt(k_ref[...], by_head_ref[...]) * head_dim ** (-0.5) + bias_ref[...]
        top = jnp.max(scores, axis=0, keepdims=True)
        weights = jnp.exp(scores - top)
        denom = jnp.sum(weights, axis=0, keepdims=True)
        w_ref[...] = (weights / denom).T

    wait(0)
    per_group = LANES // head_dim
    tall = per_group * padded

    @stage
    def _():
        project(wv_ref, v_ref)
        lane_head = lax.broadcasted_iota(jnp.int32, (padded, LANES), 1) // head_dim
        groups = []
        for g in range(width // LANES):
            weights = w_ref[g * tall : (g + 1) * tall, :]
            high = weights.astype(bf16)
            low = (weights - high.astype(f32)).astype(bf16)
            both = jnp.concatenate([high, low], axis=0)
            mixed = dot(both, v_ref[:, g * LANES : (g + 1) * LANES])
            mixed = mixed[:tall] + mixed[tall:]
            chosen = mixed[:padded]
            for h in range(1, per_group):
                chosen = jnp.where(lane_head == h, mixed[h * padded : (h + 1) * padded], chosen)
            groups.append(chosen)
        att_ref[...] = jnp.concatenate(groups, axis=1).astype(bf16)

    wait(1)
    wait(2)

    @stage
    def _():
        seq_next = (own_ref[...] + dot(att_ref[...], wo_ref[...])).astype(bf16)
        seq_wide = seq_next.astype(f32)
        projected = dot(layer_norm(seq_wide).astype(bf16), wp_ref[...]).astype(bf16).astype(f32)
        for g in range(width // LANES):
            tile = jnp.concatenate([projected, seq_wide[:, g * LANES : (g + 1) * LANES]], axis=0)
            out_ref[:, fold * g : fold * (g + 1)] = jnp.broadcast_to(
                tile.astype(bf16)[None, None], (n_row, fold) + tile.shape
            )


def update_pair(
    own, fold, chunk,
    msg_ref, mid_ref, wpair_ref, pair_ref, seq_ref,
    flat_ref, left_ref, right_ref, slab_ref,
):
    cols, rows, chans = mid_ref.shape
    n_row, n_col, twice, _ = msg_ref.shape
    half = chans // 2
    row, col = lax.axis_index("row"), lax.axis_index("col")
    flat_ref[...] = msg_ref[...].astype(f32).reshape(flat_ref.shape)
    is_first = lax.broadcasted_iota(jnp.int32, (1, chans), 1) < half

    def gathered(v, line):
        return flat_ref[pl.ds(v * n_col * twice + line, n_col, stride=twice), :]

    for q in range(own):
        at = pl.ds(q * n_col, n_col)
        left = gathered(row, q)
        left_ref[at, :] = jnp.where(is_first, left, pltpu.roll(left, half, 1))
        slab_ref[at, :] = gathered(row, twice // 2 + q)
        for v in range(n_row):
            right = gathered(v, q)
            right = jnp.where(is_first, pltpu.roll(right, half, 1), right)
            right_ref[pl.ds(v * rows + q * n_col, n_col), :] = right
    feats = LANES // fold
    turned = slab_ref[...].T
    for s in range(fold):

        @pl.when(lax.rem(col, fold) == s)
        def _():
            seq_ref[...] = turned[s * feats : (s + 1) * feats].astype(bf16)

    left = left_ref[...]

    def step(t):
        feature = []
        for j in range(chunk):
            right = right_ref[pl.ds(col * cols + t * chunk + j, 1), :]
            feature.append(jnp.where(is_first, left * right, left - right).astype(bf16))
        out = dot(jnp.concatenate(feature, axis=0), wpair_ref[...])
        here = pl.ds(t * chunk, chunk)
        mid = mid_ref[here].astype(f32)
        pair_ref[here] = (mid + out.reshape(chunk, rows, chans)).astype(bf16)

    if cols // chunk <= 4:
        for t in range(cols // chunk):
            step(t)
    else:
        pl.loop(0, cols // chunk)(step)


def local(pair, seq, w_hidden, w_back, w_bias, w_query, w_key, w_value, w_out, w_project, w_pair):
    shape = pltpu.VMEM
    rows, cols, chans = pair.shape
    length, feats = seq.shape
    width = w_query.shape[0]
    n_row, n_col = lax.axis_size("row"), lax.axis_size("col")
    fold = LANES // feats
    short = rows // fold
    plan = bias_plan(rows, cols, n_col)
    own, keys, full, rest, _, height = plan
    padded = round_up(own, 8)
    hidden_units = w_hidden.shape[1]

    chunk = max(k for k in range(1, cols + 1) if cols % k == 0 and k * rows <= 576)
    pair_mid, msg, wq = call(
        functools.partial(prepare, n_row, n_col, chunk),
        (
            shape((cols, rows, chans), bf16),
            shape((n_col, short + height, LANES), bf16),
            shape((width, width), bf16),
        ),
        [(a, "H") for a in (seq.T, w_hidden, w_back, w_bias.T, pair.transpose(1, 0, 2), w_query)],
        [
            shape((feats, length), bf16),
            shape(w_hidden.shape, bf16),
            shape(w_back.shape, bf16),
            shape(w_bias.shape[::-1], bf16),
            shape((cols, rows, chans), bf16),
            shape((cols, rows, chans), bf16),
            shape((max(full, 1), keys * n_col, LANES), f32),
            shape((keys * n_col, LANES), f32),
            pltpu.SemaphoreType.DMA((6,)),
        ],
        flops=4 * rows * cols * chans * hidden_units,
        room=24,
    )
    got = lax.all_to_all(msg, "col", split_axis=0, concat_axis=0, tiled=True)
    if n_row == 2:
        others = lax.ppermute(got, "row", [(0, 1), (1, 0)])
    else:
        others = lax.all_gather(got, "row")
    tiles = full + (1 if rest else 0)
    x_own, by_head, own_seq, bias, wk = call(
        functools.partial(own_block, plan, rows, cols),
        (
            shape((rows, width), bf16),
            shape((padded * HEADS, width), bf16),
            shape((padded, width), f32),
            shape((length, padded * HEADS), f32),
            shape((width, width), bf16),
        ),
        [(got, "V"), (wq, "V"), (w_key, "H")],
        [
            shape((rows, width), f32),
            shape((length, tiles * LANES), f32),
            pltpu.SemaphoreType.DMA((1,)),
        ],
        flops=6 * rows * width * width,
        room=16,
    )
    (out_msg,) = call(
        functools.partial(attend, rows),
        (shape((n_row, n_col, 2 * padded, LANES), bf16),),
        [(a, "V") for a in (others, x_own, by_head, own_seq, bias, wk)]
        + [(a, "H") for a in (w_value, w_out, w_project)],
        [
            shape((width, width), bf16),
            shape((width, width), bf16),
            shape(w_project.shape, bf16),
            shape((rows, width), f32),
            shape((length, width), bf16),
            shape((length, width), bf16),
            shape((length, width), bf16),
            shape((padded * HEADS, length), f32),
            shape((padded, width), bf16),
            pltpu.SemaphoreType.DMA((3,)),
        ],
        flops=6 * length * width * width,
        room=32,
    )
    flat = out_msg.reshape(n_row * n_col, 2 * padded, LANES)
    got = lax.all_to_all(flat, ("row", "col"), split_axis=0, concat_axis=0, tiled=True)
    pair_out, seq_out = call(
        functools.partial(update_pair, own, fold, chunk),
        (
            jax.ShapeDtypeStruct((cols, rows, chans), bf16),
            jax.ShapeDtypeStruct((feats, rows), bf16),
        ),
        [(a, "V") for a in (got.reshape(out_msg.shape), pair_mid, w_pair)],
        [
            shape((n_row * n_col * 2 * padded, LANES), f32),
            shape((rows, LANES), f32),
            shape((length, LANES), f32),
            shape((rows, LANES), f32),
        ],
        flops=2 * rows * cols * chans * chans,
    )
    return (pair_out.transpose(1, 0, 2), seq_out.T)


def solution(mesh):
    return jax.shard_map(
        local,
        mesh=mesh,
        in_specs=(P("row", "col", None), P(None, "col")) + (P(),) * 9,
        out_specs=(P("row", "col", None), P("row", "col")),
        check_vma=False,
    )
```

```python
import functools
import math

import jax
import jax.numpy as jnp
from jax import lax
from jax.experimental import pallas as pl
from jax.experimental.pallas import tpu as pltpu
from jax.sharding import PartitionSpec as P

HEADS = 32
LANES = 128
eps_norm = 1e-05
f32 = jnp.float32
bf16 = jnp.bfloat16


def layer_norm(values_in):
    row_mean = jnp.mean(values_in, axis=-1, keepdims=True)
    centred = values_in - row_mean
    row_var = jnp.mean(centred * centred, axis=-1, keepdims=True)
    return centred * lax.rsqrt(row_var + eps_norm)


def dot(a, b):
    return jnp.dot(a, b, preferred_element_type=f32)


def dot_nt(a, b):
    return lax.dot_general(a, b, (((1,), (1,)), ((), ())), preferred_element_type=f32)


def round_up(n, m):
    return -(-n // m) * m


def one_hot_rows(shape, target):
    rows = lax.broadcasted_iota(jnp.int32, shape, 0)
    cols = lax.broadcasted_iota(jnp.int32, shape, 1)
    return (cols == target(rows)).astype(f32).astype(bf16)


def call(kernel, outs, args, scratch=(), flops=1000, room=16):
    size = sum(a.size * a.dtype.itemsize for a, _ in args)
    size += sum(math.prod(a.shape) * jnp.dtype(a.dtype).itemsize for a in outs)
    space = {"V": pltpu.VMEM, "H": pltpu.HBM}
    return pl.pallas_call(
        kernel,
        out_shape=outs,
        in_specs=[pl.BlockSpec(memory_space=space[where]) for _, where in args],
        out_specs=tuple(pl.BlockSpec(memory_space=pltpu.VMEM) for _ in outs),
        scratch_shapes=list(scratch),
        compiler_params=pltpu.CompilerParams(vmem_limit_bytes=room * 1024 * 1024),
        cost_estimate=pl.CostEstimate(flops=flops, bytes_accessed=size, transcendentals=0),
    )(*[pltpu.with_memory_space_constraint(a, space[where]) for a, where in args])


def copies(sources, targets, sems):
    started = [
        pltpu.make_async_copy(s, t, sems.at[k]) for k, (s, t) in enumerate(zip(sources, targets))
    ]
    for one in started:
        one.start()
    return lambda k: started[k].wait()


def stage(body):
    pl.when(lax.axis_index("row") >= 0)(body)


GROUP = 4


def folded(lines):
    starts = range(0, lines.shape[0], GROUP)
    return jnp.concatenate([lines[at : at + GROUP] for at in starts], axis=1)


def lines_of(message, first, n):
    tiles = range(first // GROUP, (first + n) // GROUP)
    parts = [message(slice(t * LANES, (t + 1) * LANES)).astype(f32) for t in tiles]
    return jnp.concatenate(parts, axis=0)


def lanes_at(first, n):
    return slice(first // GROUP * LANES, (first + n) // GROUP * LANES)


def pack_seq(n_row, n_col, share, rows, seq_ref, msg_ref):
    feats = seq_ref.shape[0]
    fold = LANES // feats
    short = rows // share // fold
    row = lax.axis_index("row")
    turned = seq_ref[...].astype(f32).T
    for v in range(n_row):

        @pl.when(row == v)
        def _():
            for u in range(share):
                starts = range(v * rows + u * n_col, (v + 1) * rows, share * n_col)
                some = jnp.concatenate([turned[at : at + n_col] for at in starts], axis=0)
                tile = jnp.concatenate(
                    [some[p * short : (p + 1) * short] for p in range(fold)], axis=1
                )
                tile = folded(tile).astype(bf16)
                msg_ref[u * n_col : (u + 1) * n_col, :, lanes_at(0, short)] = jnp.broadcast_to(
                    tile[None], (n_col,) + tile.shape
                )


def bias_plan(rows, cols, n_to):
    own = rows // n_to
    keys = round_up(cols, GROUP)
    per_tile = LANES // HEADS
    full, rest = divmod(own, per_tile)
    split = per_tile // rest if rest and per_tile % rest == 0 else 1
    if rest and keys % (8 * split):
        split = 1
    height = full * keys + (keys // split if rest else 0)
    return own, keys, full, rest, split, height


def prepare(n_row, n_col, share, chunk, *refs):
    mid_ref, msg_ref, wq_ref, seq_ref, hidden_ref, back_ref, bias_ref, pair_ref = refs[6:14]
    *inner_refs, sems = refs[14:]
    wait = copies(refs[:6], (seq_ref, hidden_ref, back_ref, bias_ref, pair_ref, wq_ref), sems)
    cols, rows, chans = pair_ref.shape
    short = rows // share * seq_ref.shape[0] // LANES
    wait(0)
    pack_seq(n_row, n_col, share, rows, seq_ref, msg_ref)
    for k in range(1, 5):
        wait(k)

    @stage
    def _():
        weights = (hidden_ref, back_ref, bias_ref)
        transition(share * n_col, chunk, short, *weights, pair_ref, mid_ref, msg_ref, *inner_refs)

    wait(5)


def transition(
    n_to, chunk, short,
    hidden_ref, back_ref, bias_ref, pair_ref, mid_ref, msg_ref, norm_ref, full_ref, rest_ref,
):
    cols, rows, chans = pair_ref.shape
    own, keys, full, rest, split, height = bias_plan(rows, cols, n_to)
    per_tile = LANES // HEADS

    def step(t):
        at = t * chunk
        pair = pair_ref[pl.ds(at, chunk)].reshape(chunk * rows, chans).astype(f32)
        normed = layer_norm(pair).astype(bf16)
        hidden = jnp.maximum(dot(normed, hidden_ref[...]), 0.0).astype(bf16)
        mid = (pair + dot(hidden, back_ref[...])).astype(bf16)
        mid_ref[pl.ds(at, chunk)] = mid.reshape(chunk, rows, chans)
        normed = layer_norm(mid.astype(f32)).astype(bf16)
        norm_ref[pl.ds(at, chunk)] = normed.reshape(chunk, rows, chans)

    if cols // chunk <= 4:
        for t in range(cols // chunk):
            step(t)
    else:
        pl.loop(0, cols // chunk)(step)

    w_t = bias_ref[...]
    zero = jnp.zeros_like(w_t)
    placed = [
        jnp.concatenate([w_t if k == p else zero for k in range(per_tile)], axis=0)
        for p in range(per_tile)
    ]

    def queries(q, first, last):
        some = norm_ref[first:last, q * n_to : (q + 1) * n_to, :]
        return some.reshape((last - first) * n_to, chans)

    def wide(qs, first, last):
        return jnp.concatenate([queries(q, first, last) for q in qs], axis=1)

    for tile in range(full):
        qs = range(tile * per_tile, (tile + 1) * per_tile)
        acc = dot_nt(wide(qs, 0, cols), jnp.concatenate(placed, axis=1))
        full_ref[tile, : cols * n_to, :] = acc
        if keys > cols:
            full_ref[tile, cols * n_to :, :] = jnp.zeros(((keys - cols) * n_to, LANES), f32)
    small = keys // split
    if rest:
        qs = range(full * per_tile, own)
        for s in range(split):
            first, last = s * small, min(cols, (s + 1) * small)
            if last <= first:
                continue
            acc = dot_nt(
                wide(qs, first, last),
                jnp.concatenate(placed[s * rest : (s + 1) * rest], axis=1),
            )
            if s:
                rest_ref[: (last - first) * n_to, :] += acc
            else:
                rest_ref[: (last - first) * n_to, :] = acc
                if last < small:
                    rest_ref[last * n_to :, :] = jnp.zeros(((keys - last) * n_to, LANES), f32)
    for c in range(n_to):
        parts = [full_ref[tile, pl.ds(c, keys, stride=n_to), :] for tile in range(full)]
        if rest:
            parts.append(rest_ref[pl.ds(c, small, stride=n_to), :])
        lanes = lanes_at(short, height)
        msg_ref[c, :, lanes] = jnp.concatenate([folded(p) for p in parts], axis=1).astype(bf16)


def place(read, feats, short, x_ref, start):
    fold = LANES // feats
    slot = lax.broadcasted_iota(jnp.int32, (short, LANES), 1) // feats
    for g in range(x_ref.shape[1] // LANES):
        got = [read(fold * g + s) for s in range(fold)]
        for p in range(fold):
            piece = got[p]
            for s in range(fold):
                if s != p:
                    piece = jnp.where(
                        slot == s, pltpu.roll(got[s], (s - p) % fold * feats, 1), piece
                    )
            at = start + p * short
            x_ref[at : at + short, g * LANES : (g + 1) * LANES] = piece


def own_block(
    plan, share, cols,
    got_ref, wq_ref, wk_hbm,
    x_out, by_head_ref, own_ref, bias_ref, wk_ref,
    x_ref, raw_ref, sems,
):
    wait = copies((wk_hbm,), (wk_ref,), sems)
    own, keys, full, rest, split, _ = plan
    n_col = got_ref.shape[0] // share
    rows, width = x_ref.shape
    feats = width // n_col
    part = rows // share
    short = part * feats // LANES
    head_dim = width // HEADS
    padded = own_ref.shape[0]
    col = lax.axis_index("col")
    @stage
    def _():
        for v in range(share):
            place(
                lambda c: lines_of(lambda at: got_ref[v * n_col + c, :, at], 0, short),
                feats, short, x_ref, v * part,
            )
        normed = layer_norm(x_ref[...]).astype(bf16)
        x_out[...] = normed
        pick = one_hot_rows((padded, rows), lambda i: i * n_col + col)
        own_ref[...] = dot(pick, x_ref[...].astype(bf16))
        own_norm = dot(pick, normed).astype(bf16)

        small = keys // split
        tiles = raw_ref.shape[1] // share // LANES
        for m in range(share * n_col):
            c, lane = m % n_col, m // n_col * tiles * LANES
            read = lambda at: got_ref[m, :, at]
            for tile in range(full):
                some = lines_of(read, short + tile * keys, keys)
                raw_ref[c * cols : (c + 1) * cols, lane : lane + LANES] = some[:cols]
                lane += LANES
            if rest:
                last = lines_of(read, short + full * keys, small)
                for s in range(split):
                    height = min(small, cols - s * small)
                    if height <= 0:
                        continue
                    moved = last
                    if s:
                        moved = pltpu.roll(last, LANES - s * rest * HEADS, 1)
                    at = c * cols + s * small
                    raw_ref[at : at + height, lane : lane + LANES] = moved[:height]
        given = (raw_ref.shape[1], padded * HEADS)
        source = lax.broadcasted_iota(jnp.int32, given, 0)
        target = lax.broadcasted_iota(jnp.int32, given, 1)
        query = target % padded
        lane = query // own * (tiles * LANES) + query % own * HEADS + target // padded
        same = (source == lane) & (query < share * own)
        bias_ref[...] = dot(raw_ref[...].astype(bf16), same.astype(f32).astype(bf16))

        queries = dot(own_norm, wq_ref[...]).astype(bf16)
        spread = one_hot_rows((padded * HEADS, padded), lambda hi: hi % padded)
        wide = dot(spread, queries)
        head_of_row = lax.broadcasted_iota(jnp.int32, wide.shape, 0) // padded
        head_of_lane = lax.broadcasted_iota(jnp.int32, wide.shape, 1) // head_dim
        by_head_ref[...] = jnp.where(head_of_row == head_of_lane, wide, 0.0).astype(bf16)

    wait(0)


def attend(
    share, own, cols,
    others_ref, x_own, by_head_ref, own_ref, bias_ref, wk_ref, wv_hbm, wo_hbm, wp_hbm,
    out_ref,
    wv_ref, wo_ref, wp_ref, x_ref, xn_ref, k_ref, v_ref, w_ref, att_ref, sems,
):
    wait = copies((wv_hbm, wo_hbm, wp_hbm), (wv_ref, wo_ref, wp_ref), sems)
    n_row, n_col, lines, _ = out_ref.shape
    length, width = k_ref.shape
    rows = x_ref.shape[0]
    feats = width // n_col
    fold = LANES // feats
    part = rows // share
    short = part // fold
    head_dim = width // HEADS
    padded = own_ref.shape[0]
    row = lax.axis_index("row")

    def put(normed, v):
        for k in range(rows // n_col):
            at = k // own * rows + (k % own * share + v) * n_col
            if share == 1:
                at = v * rows + k * n_col
            xn_ref[pl.ds(pl.multiple_of(at, 16), n_col), :] = normed[k * n_col : (k + 1) * n_col]

    def block(read, v):
        for k in range(share):
            place(lambda c: read(k * n_col + c), feats, short, x_ref, k * part)
        put(layer_norm(x_ref[...]).astype(bf16), v)

    step = rows * (2 if n_row == 2 else 1)

    def project(w_of, out):
        if length == step:
            out[...] = dot(xn_ref[...], w_of[...]).astype(bf16)
        else:

            @pl.loop(0, length // step)
            def _(b):
                at = pl.ds(pl.multiple_of(b * step, 16), step)
                out[at, :] = dot(xn_ref[at, :], w_of[...]).astype(bf16)

    @stage
    def _():
        if share == 2:
            block(lambda m: lines_of(lambda at: others_ref[m, :, at], 0, short), 1 - row)
        else:

            @pl.loop(0, n_row)
            def _(v):
                block(lambda m: lines_of(lambda at: others_ref[v, m, :, at], 0, short), v)

        put(x_own[...], row)
        project(wk_ref, k_ref)
        scores = dot_nt(k_ref[...], by_head_ref[...]) * head_dim ** (-0.5) + bias_ref[...]
        top = jnp.max(scores, axis=0, keepdims=True)
        weights = jnp.exp(scores - top)
        denom = jnp.sum(weights, axis=0, keepdims=True)
        w_ref[...] = (weights / denom).T

    wait(0)
    per_group = LANES // head_dim
    tall = per_group * padded

    @stage
    def _():
        project(wv_ref, v_ref)
        lane_head = lax.broadcasted_iota(jnp.int32, (padded, LANES), 1) // head_dim
        groups = []
        for g in range(width // LANES):
            weights = w_ref[g * tall : (g + 1) * tall, :]
            high = weights.astype(bf16)
            low = (weights - high.astype(f32)).astype(bf16)
            both = jnp.concatenate([high, low], axis=0)
            mixed = dot(both, v_ref[:, g * LANES : (g + 1) * LANES])
            mixed = mixed[:tall] + mixed[tall:]
            chosen = mixed[:padded]
            for h in range(1, per_group):
                chosen = jnp.where(lane_head == h, mixed[h * padded : (h + 1) * padded], chosen)
            groups.append(chosen)
        att_ref[...] = jnp.concatenate(groups, axis=1).astype(bf16)

    wait(1)
    wait(2)

    @stage
    def _():
        seq_next = (own_ref[...] + dot(att_ref[...], wo_ref[...])).astype(bf16)
        seq_wide = seq_next.astype(f32)
        projected = dot(layer_norm(seq_wide).astype(bf16), wp_ref[...]).astype(bf16).astype(f32)
        is_left = lax.broadcasted_iota(jnp.int32, (own, LANES), 1) < LANES // 2
        rest = jnp.zeros((lines - 2 * own, LANES), f32)
        for v in range(n_row):
            to = v * own if share == n_row else 0
            for c in range(n_col):
                of = c * cols // rows * own if share == n_row else 0
                sides = jnp.where(
                    is_left, projected[to : to + own], projected[of : of + own]
                )
                g = c // fold * LANES
                slab = seq_wide[to : to + own, g : g + LANES]
                out_ref[v, c] = jnp.concatenate([sides, slab, rest], axis=0).astype(bf16)


def update_pair(
    share, own, fold, chunk,
    msg_ref, mid_ref, wpair_ref, pair_ref, seq_ref,
    flat_ref, left_ref, right_ref, slab_ref,
):
    cols, rows, chans = mid_ref.shape
    n_row, n_col, lines, _ = msg_ref.shape
    n_from = share * n_col
    half = chans // 2
    row, col = lax.axis_index("row"), lax.axis_index("col")
    flat_ref[...] = msg_ref[...].astype(f32).reshape(flat_ref.shape)
    is_first = lax.broadcasted_iota(jnp.int32, (1, chans), 1) < half

    def gathered(v, line):
        first = 0 if share == n_row else v * n_col * lines
        return flat_ref[pl.ds(first + line, n_from, stride=lines), :]

    for q in range(own):
        at = pl.ds(q * n_from, n_from)
        left = gathered(row, q)
        left_ref[at, :] = jnp.where(is_first, left, pltpu.roll(left, half, 1))
        slab_ref[at, :] = gathered(row, own + q)
        for v in range(right_ref.shape[0] // rows):
            right = gathered(v, q)
            right = jnp.where(is_first, pltpu.roll(right, half, 1), right)
            right_ref[pl.ds(v * rows + q * n_from, n_from), :] = right
    first_key = lax.rem(col * cols, right_ref.shape[0])
    feats = LANES // fold
    turned = slab_ref[...].T
    for s in range(fold):

        @pl.when(lax.rem(col, fold) == s)
        def _():
            seq_ref[...] = turned[s * feats : (s + 1) * feats].astype(bf16)

    left = left_ref[...]

    def step(t):
        feature = []
        for j in range(chunk):
            right = right_ref[pl.ds(first_key + t * chunk + j, 1), :]
            feature.append(jnp.where(is_first, left * right, left - right).astype(bf16))
        out = dot(jnp.concatenate(feature, axis=0), wpair_ref[...])
        here = pl.ds(t * chunk, chunk)
        mid = mid_ref[here].astype(f32)
        pair_ref[here] = (mid + out.reshape(chunk, rows, chans)).astype(bf16)

    if cols // chunk <= 4:
        for t in range(cols // chunk):
            step(t)
    else:
        pl.loop(0, cols // chunk)(step)


def local(pair, seq, w_hidden, w_back, w_bias, w_query, w_key, w_value, w_out, w_project, w_pair):
    shape = pltpu.VMEM
    rows, cols, chans = pair.shape
    length, feats = seq.shape
    width = w_query.shape[0]
    n_row, n_col = lax.axis_size("row"), lax.axis_size("col")
    fold = LANES // feats
    share = 2 if n_row == 2 and rows % (2 * n_col) == 0 and rows % (16 * fold) == 0 else 1
    n_to = share * n_col
    everyone = ("row", "col") if share == n_row else "col"
    short = rows // share // fold
    plan = bias_plan(rows, cols, n_to)
    own, keys, full, rest, _, height = plan
    padded = round_up(share * own, 8)
    lines = round_up(2 * own, 8)
    hidden_units = w_hidden.shape[1]

    chunk = max(k for k in range(1, cols + 1) if cols % k == 0 and k * rows <= 576)
    pair_mid, msg, wq = call(
        functools.partial(prepare, n_row, n_col, share, chunk),
        (
            shape((cols, rows, chans), bf16),
            shape((n_to, GROUP, (short + height) // GROUP * LANES), bf16),
            shape((width, width), bf16),
        ),
        [(a, "H") for a in (seq.T, w_hidden, w_back, w_bias.T, pair.transpose(1, 0, 2), w_query)],
        [
            shape((feats, length), bf16),
            shape(w_hidden.shape, bf16),
            shape(w_back.shape, bf16),
            shape(w_bias.shape[::-1], bf16),
            shape((cols, rows, chans), bf16),
            shape((cols, rows, chans), bf16),
            shape((max(full, 1), keys * n_to, LANES), f32),
            shape((keys * n_to, LANES), f32),
            pltpu.SemaphoreType.DMA((6,)),
        ],
        flops=4 * rows * cols * chans * hidden_units,
        room=24,
    )
    got = lax.all_to_all(msg, everyone, split_axis=0, concat_axis=0, tiled=True)
    if share == 2:
        others = lax.ppermute(got, "row", [(0, 1), (1, 0)])
    else:
        others = lax.all_gather(got, "row")
    tiles = full + (1 if rest else 0)
    x_own, by_head, own_seq, bias, wk = call(
        functools.partial(own_block, plan, share, cols),
        (
            shape((rows, width), bf16),
            shape((padded * HEADS, width), bf16),
            shape((padded, width), f32),
            shape((length, padded * HEADS), f32),
            shape((width, width), bf16),
        ),
        [(got, "V"), (wq, "V"), (w_key, "H")],
        [
            shape((rows, width), f32),
            shape((length, share * tiles * LANES), f32),
            pltpu.SemaphoreType.DMA((1,)),
        ],
        flops=6 * rows * width * width,
        room=16,
    )
    (out_msg,) = call(
        functools.partial(attend, share, own, cols),
        (shape((n_row, n_col, lines, LANES), bf16),),
        [(a, "V") for a in (others, x_own, by_head, own_seq, bias, wk)]
        + [(a, "H") for a in (w_value, w_out, w_project)],
        [
            shape((width, width), bf16),
            shape((width, width), bf16),
            shape(w_project.shape, bf16),
            shape((rows, width), f32),
            shape((length, width), bf16),
            shape((length, width), bf16),
            shape((length, width), bf16),
            shape((padded * HEADS, length), f32),
            shape((padded, width), bf16),
            pltpu.SemaphoreType.DMA((3,)),
        ],
        flops=6 * length * width * width,
        room=32,
    )
    flat = out_msg.reshape(n_row * n_col, lines, LANES)
    got = lax.all_to_all(flat, ("row", "col"), split_axis=0, concat_axis=0, tiled=True)
    pair_out, seq_out = call(
        functools.partial(update_pair, share, own, fold, chunk),
        (
            jax.ShapeDtypeStruct((cols, rows, chans), bf16),
            jax.ShapeDtypeStruct((feats, rows), bf16),
        ),
        [(a, "V") for a in (got.reshape(out_msg.shape), pair_mid, w_pair)],
        [
            shape((n_row * n_col * lines, LANES), f32),
            shape((rows, LANES), f32),
            shape((rows if share == n_row else length, LANES), f32),
            shape((rows, LANES), f32),
        ],
        flops=2 * rows * cols * chans * chans,
    )
    return (pair_out.transpose(1, 0, 2), seq_out.T)


def solution(mesh):
    return jax.shard_map(
        local,
        mesh=mesh,
        in_specs=(P("row", "col", None), P(None, "col")) + (P(),) * 9,
        out_specs=(P("row", "col", None), P("row", "col")),
        check_vma=False,
    )
```

```python
import functools
import math

import jax
import jax.numpy as jnp
from jax import lax
from jax.experimental import pallas as pl
from jax.experimental.pallas import tpu as pltpu
from jax.sharding import PartitionSpec as P

HEADS = 32
LANES = 128
eps_norm = 1e-05
f32 = jnp.float32
bf16 = jnp.bfloat16


def layer_norm(values_in):
    row_mean = jnp.mean(values_in, axis=-1, keepdims=True)
    centred = values_in - row_mean
    row_var = jnp.mean(centred * centred, axis=-1, keepdims=True)
    return centred * lax.rsqrt(row_var + eps_norm)


def dot(a, b):
    return jnp.dot(a, b, preferred_element_type=f32)


def dot_nt(a, b):
    return lax.dot_general(a, b, (((1,), (1,)), ((), ())), preferred_element_type=f32)


def round_up(n, m):
    return -(-n // m) * m


def one_hot_rows(shape, target):
    rows = lax.broadcasted_iota(jnp.int32, shape, 0)
    cols = lax.broadcasted_iota(jnp.int32, shape, 1)
    return (cols == target(rows)).astype(f32).astype(bf16)


def call(kernel, outs, args, scratch=(), flops=1000, room=16):
    size = sum(a.size * a.dtype.itemsize for a, _ in args)
    size += sum(math.prod(a.shape) * jnp.dtype(a.dtype).itemsize for a in outs)
    space = {"V": pltpu.VMEM, "H": pltpu.HBM}
    return pl.pallas_call(
        kernel,
        out_shape=outs,
        in_specs=[pl.BlockSpec(memory_space=space[where]) for _, where in args],
        out_specs=tuple(pl.BlockSpec(memory_space=pltpu.VMEM) for _ in outs),
        scratch_shapes=list(scratch),
        compiler_params=pltpu.CompilerParams(vmem_limit_bytes=room * 1024 * 1024),
        cost_estimate=pl.CostEstimate(flops=flops, bytes_accessed=size, transcendentals=0),
    )(*[pltpu.with_memory_space_constraint(a, space[where]) for a, where in args])


def copies(sources, targets, sems):
    started = [
        pltpu.make_async_copy(s, t, sems.at[k]) for k, (s, t) in enumerate(zip(sources, targets))
    ]
    for one in started:
        one.start()
    return lambda k: started[k].wait()


def stage(body):
    pl.when(lax.axis_index("row") >= 0)(body)


GROUP = 2


def folded(lines, group=GROUP):
    starts = range(0, lines.shape[0], group)
    return jnp.concatenate([lines[at : at + group] for at in starts], axis=1)


def lines_of(message, first, n):
    tiles = range(first // GROUP, (first + n) // GROUP)
    parts = [message(slice(t * LANES, (t + 1) * LANES)).astype(f32) for t in tiles]
    return jnp.concatenate(parts, axis=0)


def lanes_at(first, n):
    return slice(first // GROUP * LANES, (first + n) // GROUP * LANES)


def pack_seq(n_row, n_col, share, rows, seq_ref, msg_ref):
    feats = seq_ref.shape[0]
    fold = LANES // feats
    short = rows // share // fold
    row = lax.axis_index("row")
    turned = seq_ref[...].astype(f32).T
    for v in range(n_row):

        @pl.when(row == v)
        def _():
            for u in range(share):
                starts = range(v * rows + u * n_col, (v + 1) * rows, share * n_col)
                some = jnp.concatenate([turned[at : at + n_col] for at in starts], axis=0)
                tile = jnp.concatenate(
                    [some[p * short : (p + 1) * short] for p in range(fold)], axis=1
                )
                tile = folded(tile).astype(bf16)
                msg_ref[u * n_col : (u + 1) * n_col, :, lanes_at(0, short)] = jnp.broadcast_to(
                    tile[None], (n_col,) + tile.shape
                )


def bias_plan(rows, cols, n_to):
    own = rows // n_to
    keys = round_up(cols, GROUP)
    per_tile = LANES // HEADS
    full, rest = divmod(own, per_tile)
    split = per_tile // rest if rest and per_tile % rest == 0 else 1
    if rest and keys % (8 * split):
        split = 1
    height = full * keys + (keys // split if rest else 0)
    base = 0
    if full == 0 and rest == per_tile - 1 and cols % per_tile == 0:
        base = cols // per_tile * rest
        height = round_up(base, GROUP)
    return own, keys, full, rest, split, height, base


def prepare(n_row, n_col, share, chunk, *refs):
    mid_ref, msg_ref, wq_ref, wva_ref, seq_ref, hidden_ref, back_ref, bias_ref, pair_ref = refs[7:16]
    *inner_refs, sems = refs[16:]
    wait = copies(
        refs[:6] + (refs[6].at[:, pl.ds(0, wva_ref.shape[1])],),
        (seq_ref, hidden_ref, back_ref, bias_ref, pair_ref, wq_ref, wva_ref),
        sems,
    )
    cols, rows, chans = pair_ref.shape
    short = rows // share * seq_ref.shape[0] // LANES
    wait(0)
    pack_seq(n_row, n_col, share, rows, seq_ref, msg_ref)
    for k in range(1, 5):
        wait(k)

    @stage
    def _():
        weights = (hidden_ref, back_ref, bias_ref)
        transition(share * n_col, chunk, short, *weights, pair_ref, mid_ref, msg_ref, *inner_refs)

    wait(5)
    wait(6)


def transition(
    n_to, chunk, short,
    hidden_ref, back_ref, bias_ref, pair_ref, mid_ref, msg_ref, norm_ref, full_ref, rest_ref,
):
    cols, rows, chans = pair_ref.shape
    own, keys, full, rest, split, height, base = bias_plan(rows, cols, n_to)
    per_tile = LANES // HEADS

    def step(t):
        at = t * chunk
        pair = pair_ref[pl.ds(at, chunk)].reshape(chunk * rows, chans).astype(f32)
        normed = layer_norm(pair).astype(bf16)
        hidden = jnp.maximum(dot(normed, hidden_ref[...]), 0.0).astype(bf16)
        mid = (pair + dot(hidden, back_ref[...])).astype(bf16)
        mid_ref[pl.ds(at, chunk)] = mid.reshape(chunk, rows, chans)
        normed = layer_norm(mid.astype(f32)).astype(bf16)
        norm_ref[pl.ds(at, chunk)] = normed.reshape(chunk, rows, chans)

    if cols // chunk <= 4:
        for t in range(cols // chunk):
            step(t)
    else:
        pl.loop(0, cols // chunk)(step)

    w_t = bias_ref[...]
    zero = jnp.zeros_like(w_t)
    placed = [
        jnp.concatenate([w_t if k == p else zero for k in range(per_tile)], axis=0)
        for p in range(per_tile)
    ]

    def queries(q, first, last):
        some = norm_ref[first:last, q * n_to : (q + 1) * n_to, :]
        return some.reshape((last - first) * n_to, chans)

    def wide(qs, first, last):
        return jnp.concatenate([queries(q, first, last) for q in qs], axis=1)

    for tile in range(full):
        qs = range(tile * per_tile, (tile + 1) * per_tile)
        acc = dot_nt(wide(qs, 0, cols), jnp.concatenate(placed, axis=1))
        full_ref[tile, : cols * n_to, :] = acc
        if keys > cols:
            full_ref[tile, cols * n_to :, :] = jnp.zeros(((keys - cols) * n_to, LANES), f32)
    small = keys // split
    if base:
        small = height
        lines = [(base + m, q) for m in range(cols - base) for q in range(rest)]
        sides = [queries(q, 0, base) for q in range(rest)]
        sides.append(jnp.concatenate([queries(q, k, k + 1) for k, q in lines], axis=0))
        acc = dot_nt(jnp.concatenate(sides, axis=1), jnp.concatenate(placed, axis=1))
        rest_ref[: base * n_to, :] = acc
        if height > base:
            rest_ref[base * n_to : height * n_to, :] = jnp.zeros(
                ((height - base) * n_to, LANES), f32
            )
    elif rest:
        qs = range(full * per_tile, own)
        for s in range(split):
            first, last = s * small, min(cols, (s + 1) * small)
            if last <= first:
                continue
            acc = dot_nt(
                wide(qs, first, last),
                jnp.concatenate(placed[s * rest : (s + 1) * rest], axis=1),
            )
            if s:
                rest_ref[: (last - first) * n_to, :] += acc
            else:
                rest_ref[: (last - first) * n_to, :] = acc
                if last < small:
                    rest_ref[last * n_to :, :] = jnp.zeros(((keys - last) * n_to, LANES), f32)
    for c in range(n_to):
        parts = [full_ref[tile, pl.ds(c, keys, stride=n_to), :] for tile in range(full)]
        if rest:
            parts.append(rest_ref[pl.ds(c, small, stride=n_to), :])
        lanes = lanes_at(short, height)
        msg_ref[c, :, lanes] = jnp.concatenate([folded(p) for p in parts], axis=1).astype(bf16)


def place(read, feats, short, x_ref, start):
    fold = LANES // feats
    slot = lax.broadcasted_iota(jnp.int32, (short, LANES), 1) // feats
    for g in range(x_ref.shape[1] // LANES):
        got = [read(fold * g + s) for s in range(fold)]
        for p in range(fold):
            piece = got[p]
            for s in range(fold):
                if s != p:
                    piece = jnp.where(
                        slot == s, pltpu.roll(got[s], (s - p) % fold * feats, 1), piece
                    )
            at = start + p * short
            x_ref[at : at + short, g * LANES : (g + 1) * LANES] = piece


def own_block(
    plan, share, cols,
    got_ref, wq_ref, wk_hbm, wv_hbm,
    x_out, by_head_ref, own_ref, bias_ref, wk_ref, wvb_ref,
    x_ref, raw_ref, sems,
):
    ahead = wvb_ref.shape[1]
    wait = copies((wk_hbm, wv_hbm.at[:, pl.ds(ahead, ahead)]), (wk_ref, wvb_ref), sems)
    own, keys, full, rest, split, height, base = plan
    n_col = got_ref.shape[0] // share
    rows, width = x_ref.shape
    feats = width // n_col
    part = rows // share
    short = part * feats // LANES
    head_dim = width // HEADS
    padded = own_ref.shape[0]
    col = lax.axis_index("col")
    @stage
    def _():
        for v in range(share):
            place(
                lambda c: lines_of(lambda at: got_ref[v * n_col + c, :, at], 0, short),
                feats, short, x_ref, v * part,
            )
        normed = layer_norm(x_ref[...]).astype(bf16)
        x_out[...] = normed
        pick = one_hot_rows((padded, rows), lambda i: i * n_col + col)
        own_ref[...] = dot(pick, x_ref[...].astype(bf16))
        own_norm = dot(pick, normed).astype(bf16)

        small = keys // split
        tiles = raw_ref.shape[1] // share // LANES
        for m in range(share * n_col):
            c, lane = m % n_col, m // n_col * tiles * LANES
            read = lambda at: got_ref[m, :, at]
            if base:
                some = lines_of(read, short, height)
                raw_ref[c * base : (c + 1) * base, lane : lane + LANES] = some[:base]
                continue
            for tile in range(full):
                some = lines_of(read, short + tile * keys, keys)
                raw_ref[c * cols : (c + 1) * cols, lane : lane + LANES] = some[:cols]
                lane += LANES
            if rest:
                last = lines_of(read, short + full * keys, small)
                for s in range(split):
                    some = min(small, cols - s * small)
                    if some <= 0:
                        continue
                    moved = last
                    if s:
                        moved = pltpu.roll(last, LANES - s * rest * HEADS, 1)
                    at = c * cols + s * small
                    raw_ref[at : at + some, lane : lane + LANES] = moved[:some]
        given = (raw_ref.shape[1], padded * HEADS)
        source = lax.broadcasted_iota(jnp.int32, given, 0)
        target = lax.broadcasted_iota(jnp.int32, given, 1)
        query = target % padded
        lane = query // own * (tiles * LANES) + query % own * HEADS + target // padded
        same = (source == lane) & (query < share * own)
        one_hot = lambda where: where.astype(f32).astype(bf16)
        if base:
            raw = raw_ref[: n_col * base, :].astype(bf16)
            last = (query // own * LANES + rest * HEADS + target // padded == source) & (
                query < share * own
            )
            early = dot(raw, one_hot(same)).astype(bf16)
            late = dot(raw, one_hot(last)).astype(bf16)
            which = (n_col * cols, n_col * base)
            key = lax.broadcasted_iota(jnp.int32, which, 0)
            line = lax.broadcasted_iota(jnp.int32, which, 1)
            j = key % cols
            begin = key // cols * base
            total = dot(one_hot((j < base) & (line == begin + j)), early)
            slot = lax.broadcasted_iota(jnp.int32, total.shape, 1) % padded % own
            for q in range(own):
                chosen = (j >= base) & (line == begin + (j - base) * own + q)
                total = total + jnp.where(slot == q, dot(one_hot(chosen), late), 0.0)
            bias_ref[...] = total
        else:
            bias_ref[...] = dot(raw_ref[...].astype(bf16), one_hot(same))

        queries = dot(own_norm, wq_ref[...]).astype(bf16)
        spread = one_hot_rows((padded * HEADS, padded), lambda hi: hi % padded)
        wide = dot(spread, queries)
        head_of_row = lax.broadcasted_iota(jnp.int32, wide.shape, 0) // padded
        head_of_lane = lax.broadcasted_iota(jnp.int32, wide.shape, 1) // head_dim
        by_head_ref[...] = jnp.where(head_of_row == head_of_lane, wide, 0.0).astype(bf16)

    wait(0)
    wait(1)


def attend(
    share, own, cols,
    others_ref, x_own, by_head_ref, own_ref, bias_ref, wk_ref, wva_ref, wvb_ref, wv_hbm, wo_hbm, wp_hbm,
    out_ref,
    wv_ref, wo_ref, wp_ref, x_ref, xn_ref, k_ref, v_ref, w_ref, att_ref, sems,
):
    ahead = wva_ref.shape[1]
    last = wv_hbm.at[:, pl.ds(2 * ahead, wv_ref.shape[1])]
    wait = copies((last, wo_hbm, wp_hbm), (wv_ref, wo_ref, wp_ref), sems)
    n_row, n_col, pairs, _ = out_ref.shape
    length, width = k_ref.shape
    rows = x_ref.shape[0]
    feats = width // n_col
    fold = LANES // feats
    part = rows // share
    short = part // fold
    head_dim = width // HEADS
    padded = own_ref.shape[0]
    row = lax.axis_index("row")

    def put(normed, v):
        for k in range(rows // n_col):
            at = k // own * rows + (k % own * share + v) * n_col
            if share == 1:
                at = v * rows + k * n_col
            xn_ref[pl.ds(pl.multiple_of(at, 16), n_col), :] = normed[k * n_col : (k + 1) * n_col]

    def block(read, v):
        for k in range(share):
            place(lambda c: read(k * n_col + c), feats, short, x_ref, k * part)
        put(layer_norm(x_ref[...]).astype(bf16), v)

    step = rows * (2 if n_row == 2 else 1)

    def project(w_of, out, first=0):
        lanes = pl.ds(first, w_of.shape[1])
        if length == step:
            out[:, lanes] = dot(xn_ref[...], w_of[...]).astype(bf16)
        else:

            @pl.loop(0, length // step)
            def _(b):
                at = pl.ds(pl.multiple_of(b * step, 16), step)
                out[at, lanes] = dot(xn_ref[at, :], w_of[...]).astype(bf16)

    @stage
    def _():
        if share == 2:
            block(lambda m: lines_of(lambda at: others_ref[m, :, at], 0, short), 1 - row)
        else:

            @pl.loop(0, n_row)
            def _(v):
                block(lambda m: lines_of(lambda at: others_ref[v, m, :, at], 0, short), v)

        put(x_own[...], row)
        project(wk_ref, k_ref)
        scores = dot_nt(k_ref[...], by_head_ref[...]) * head_dim ** (-0.5) + bias_ref[...]
        top = jnp.max(scores, axis=0, keepdims=True)
        weights = jnp.exp(scores - top)
        denom = jnp.sum(weights, axis=0, keepdims=True)
        w_ref[...] = (weights / denom).T
        project(wva_ref, v_ref)
        project(wvb_ref, v_ref, ahead)

    wait(0)
    per_group = LANES // head_dim
    tall = per_group * padded

    @stage
    def _():
        project(wv_ref, v_ref, 2 * ahead)
        lane_head = lax.broadcasted_iota(jnp.int32, (padded, LANES), 1) // head_dim
        groups = []
        for g in range(width // LANES):
            weights = w_ref[g * tall : (g + 1) * tall, :]
            high = weights.astype(bf16)
            low = (weights - high.astype(f32)).astype(bf16)
            both = jnp.concatenate([high, low], axis=0)
            mixed = dot(both, v_ref[:, g * LANES : (g + 1) * LANES])
            mixed = mixed[:tall] + mixed[tall:]
            chosen = mixed[:padded]
            for h in range(1, per_group):
                chosen = jnp.where(lane_head == h, mixed[h * padded : (h + 1) * padded], chosen)
            groups.append(chosen)
        att_ref[...] = jnp.concatenate(groups, axis=1).astype(bf16)

    wait(1)
    wait(2)

    @stage
    def _():
        seq_next = (own_ref[...] + dot(att_ref[...], wo_ref[...])).astype(bf16)
        seq_wide = seq_next.astype(f32)
        projected = dot(layer_norm(seq_wide).astype(bf16), wp_ref[...]).astype(bf16).astype(f32)
        is_left = lax.broadcasted_iota(jnp.int32, (own, LANES), 1) < LANES // 2
        for v in range(n_row):
            to = v * own if share == n_row else 0
            for c in range(n_col):
                of = c * cols // rows * own if share == n_row else 0
                sides = jnp.where(
                    is_left, projected[to : to + own], projected[of : of + own]
                )
                g = c // fold * LANES
                slab = seq_wide[to : to + own, g : g + LANES]
                tile = jnp.concatenate([sides, slab], axis=0)
                out_ref[v, c] = folded(tile, pairs).astype(bf16)


def update_pair(
    share, own, fold, chunk,
    msg_ref, mid_ref, wpair_ref, pair_ref, seq_ref,
    flat_ref, left_ref, right_ref, slab_ref,
):
    cols, rows, chans = mid_ref.shape
    n_row, n_col, pairs, _ = msg_ref.shape
    n_from = share * n_col
    half = chans // 2
    row, col = lax.axis_index("row"), lax.axis_index("col")
    for m in range(n_row * n_col):
        message = msg_ref[m // n_col, m % n_col].astype(f32)
        for t in range(own):
            flat_ref[t, m * pairs : (m + 1) * pairs, :] = message[:, t * LANES : (t + 1) * LANES]
    is_first = lax.broadcasted_iota(jnp.int32, (1, chans), 1) < half

    def gathered(v, line):
        first = 0 if share == n_row else v * n_col * pairs
        return flat_ref[line // pairs, pl.ds(first + line % pairs, n_from, stride=pairs), :]

    for q in range(own):
        at = pl.ds(q * n_from, n_from)
        left = gathered(row, q)
        left_ref[at, :] = jnp.where(is_first, left, pltpu.roll(left, half, 1))
        slab_ref[at, :] = gathered(row, own + q)
        for v in range(right_ref.shape[0] // rows):
            right = gathered(v, q)
            right = jnp.where(is_first, pltpu.roll(right, half, 1), right)
            right_ref[pl.ds(v * rows + q * n_from, n_from), :] = right
    first_key = lax.rem(col * cols, right_ref.shape[0])
    feats = LANES // fold
    turned = slab_ref[...].T
    for s in range(fold):

        @pl.when(lax.rem(col, fold) == s)
        def _():
            seq_ref[...] = turned[s * feats : (s + 1) * feats].astype(bf16)

    left = left_ref[...]

    def step(t):
        feature = []
        for j in range(chunk):
            right = right_ref[pl.ds(first_key + t * chunk + j, 1), :]
            feature.append(jnp.where(is_first, left * right, left - right).astype(bf16))
        out = dot(jnp.concatenate(feature, axis=0), wpair_ref[...])
        here = pl.ds(t * chunk, chunk)
        mid = mid_ref[here].astype(f32)
        pair_ref[here] = (mid + out.reshape(chunk, rows, chans)).astype(bf16)

    if cols // chunk <= 4:
        for t in range(cols // chunk):
            step(t)
    else:
        pl.loop(0, cols // chunk)(step)


def local(pair, seq, w_hidden, w_back, w_bias, w_query, w_key, w_value, w_out, w_project, w_pair):
    shape = pltpu.VMEM
    rows, cols, chans = pair.shape
    length, feats = seq.shape
    width = w_query.shape[0]
    n_row, n_col = lax.axis_size("row"), lax.axis_size("col")
    fold = LANES // feats
    share = 2 if n_row == 2 and rows % (2 * n_col) == 0 and rows % (16 * fold) == 0 else 1
    n_to = share * n_col
    everyone = ("row", "col") if share == n_row else "col"
    short = rows // share // fold
    plan = bias_plan(rows, cols, n_to)
    own, keys, full, rest, _, height, _ = plan
    padded = round_up(share * own, 8)
    pairs, tiles_out = 2, own
    hidden_units = w_hidden.shape[1]

    chunk = max(k for k in range(1, cols + 1) if cols % k == 0 and k * rows <= 576)
    ahead = width // 4
    pair_mid, msg, wq, wva = call(
        functools.partial(prepare, n_row, n_col, share, chunk),
        (
            shape((cols, rows, chans), bf16),
            shape((n_to, GROUP, (short + height) // GROUP * LANES), bf16),
            shape((width, width), bf16),
            shape((width, ahead), bf16),
        ),
        [
            (a, "H")
            for a in (seq.T, w_hidden, w_back, w_bias.T, pair.transpose(1, 0, 2), w_query, w_value)
        ],
        [
            shape((feats, length), bf16),
            shape(w_hidden.shape, bf16),
            shape(w_back.shape, bf16),
            shape(w_bias.shape[::-1], bf16),
            shape((cols, rows, chans), bf16),
            shape((cols, rows, chans), bf16),
            shape((max(full, 1), keys * n_to, LANES), f32),
            shape((keys * n_to, LANES), f32),
            pltpu.SemaphoreType.DMA((7,)),
        ],
        flops=4 * rows * cols * chans * hidden_units,
        room=24,
    )
    got = lax.all_to_all(msg, everyone, split_axis=0, concat_axis=0, tiled=True)
    if share == 2:
        others = lax.ppermute(got, "row", [(0, 1), (1, 0)])
    else:
        others = lax.all_gather(got, "row")
    tiles = full + (1 if rest else 0)
    x_own, by_head, own_seq, bias, wk, wvb = call(
        functools.partial(own_block, plan, share, cols),
        (
            shape((rows, width), bf16),
            shape((padded * HEADS, width), bf16),
            shape((padded, width), f32),
            shape((length, padded * HEADS), f32),
            shape((width, width), bf16),
            shape((width, ahead), bf16),
        ),
        [(got, "V"), (wq, "V"), (w_key, "H"), (w_value, "H")],
        [
            shape((rows, width), f32),
            shape((length, share * tiles * LANES), f32),
            pltpu.SemaphoreType.DMA((2,)),
        ],
        flops=6 * rows * width * width,
        room=16,
    )
    (out_msg,) = call(
        functools.partial(attend, share, own, cols),
        (shape((n_row, n_col, pairs, tiles_out * LANES), bf16),),
        [(a, "V") for a in (others, x_own, by_head, own_seq, bias, wk, wva, wvb)]
        + [(a, "H") for a in (w_value, w_out, w_project)],
        [
            shape((width, width - 2 * ahead), bf16),
            shape((width, width), bf16),
            shape(w_project.shape, bf16),
            shape((rows, width), f32),
            shape((length, width), bf16),
            shape((length, width), bf16),
            shape((length, width), bf16),
            shape((padded * HEADS, length), f32),
            shape((padded, width), bf16),
            pltpu.SemaphoreType.DMA((3,)),
        ],
        flops=6 * length * width * width,
        room=32,
    )
    flat = out_msg.reshape(n_row * n_col, pairs, tiles_out * LANES)
    got = lax.all_to_all(flat, ("row", "col"), split_axis=0, concat_axis=0, tiled=True)
    pair_out, seq_out = call(
        functools.partial(update_pair, share, own, fold, chunk),
        (
            jax.ShapeDtypeStruct((cols, rows, chans), bf16),
            jax.ShapeDtypeStruct((feats, rows), bf16),
        ),
        [(a, "V") for a in (got.reshape(out_msg.shape), pair_mid, w_pair)],
        [
            shape((tiles_out, n_row * n_col * pairs, LANES), f32),
            shape((rows, LANES), f32),
            shape((rows if share == n_row else length, LANES), f32),
            shape((rows, LANES), f32),
        ],
        flops=2 * rows * cols * chans * chans,
    )
    return (pair_out.transpose(1, 0, 2), seq_out.T)


def solution(mesh):
    return jax.shard_map(
        local,
        mesh=mesh,
        in_specs=(P("row", "col", None), P(None, "col")) + (P(),) * 9,
        out_specs=(P("row", "col", None), P("row", "col")),
        check_vma=False,
    )
```
